1024 devices in a mesh: hst: 8 (over y_lo, core), outer: 128 (over z, x, y_hi).
Axes of the slice: x: 4, y: 8 (y_hi: 2, y_lo: 4; y = y_hi * 4 + y_lo), z: 16, core: 2. Of those that a mesh axis runs over, the one named last changes fastest.
Arguments:
- tokens: bfloat16 [131072, 4096], P(('hst', 'outer')), may hold values from -24 to 24
- weight_codes: int32 [4096, 512], P('hst'), may hold values from -127 to 127
- weight_scales: float32 [32, 512], P('hst'), may hold values from 0.0001 to 0.0006
- grad_codes: int32 [131072, 512], P(('hst', 'outer')), may hold values from -8 to 7
- grad_scales: float32 [131072, 4], P(('hst', 'outer')), may hold values from 0.05 to 0.5
Outputs:
- values: bfloat16 [131072, 512], P(('hst', 'outer'))
- tokens_grad: bfloat16 [131072, 4096], P(('hst', 'outer'))
- weight_grad: float32 [4096, 512], P(('hst', 'outer'))
The draws below stay inside these ranges and needn't reach their ends.
All inputs are finite; a program needn't handle non-finite values.
Results may differ from the reference program's by a relative error of at most 0.015.
Values may be sent and summed in bfloat16 or wider, within the bound.
A program may use at most 64 MiB of HBM per device.

```python
import math
import jax
import jax.numpy as jnp
from jax import lax

D = 4096
HEADS_KV = 4
HEAD_DIM = 128
BLOCK = 128
TOK_DEV = 128
KV = 512
TOKENS = 131072
N_HST = 8
N_OUTER = 128


def plant(array, stream_key, low, high):
    longest = array.shape.index(max(array.shape))
    spots = []
    for shift in (0, 1):
        where = [jax.random.randint(jax.random.fold_in(stream_key, axis), (), 0, length) for axis, length in enumerate(array.shape)]
        where[longest] = (where[longest] + shift) % array.shape[longest]
        spots.append(tuple(where))
    return array.at[spots[0]].set(low).at[spots[1]].set(high)


def spiked(result, rng, source, target, shards_of, factor):
    def block_of(dim):
        return (jnp.arange(result.shape[dim]) // (result.shape[dim] // shards_of)).reshape((-1,) + (1,) * (result.ndim - 1 - dim))

    first = jax.random.permutation(rng, shards_of)[block_of(target)]
    second = (block_of(target) + shards_of // 2) % shards_of
    return jnp.where((block_of(source) == first) | (block_of(source) == second), factor * result, result)


def block_levels(stream_key, extent, pieces, smallest, high):
    def one(dim, parts):
        heights = jax.random.uniform(jax.random.fold_in(jax.random.fold_in(stream_key, 6), dim), (parts,), jnp.float32, smallest / len(pieces), high / len(pieces))
        return jnp.repeat(jnp.exp(heights), extent[dim] // parts).reshape((-1,) + (1,) * (len(extent) - dim - 1))

    gain = one(*pieces[0])
    for cut in pieces[1:]:
        gain = gain * one(*cut)
    return gain


def noise_with(own_key, extent, spread, bound, pieces, heavy, dtype=jnp.bfloat16):
    result = spread * jax.random.normal(own_key, extent, jnp.float32)
    if pieces:
        result = result * block_levels(own_key, extent, pieces, -0.22, 0.18)
    return jnp.clip(spiked(result, jax.random.fold_in(own_key, 3), *heavy), -bound, bound).astype(dtype)


def setup_inputs(seed: int = 0) -> dict:
    seeds = jax.random.split(jax.random.key(seed), 6)
    tokens = noise_with(seeds[0], (TOKENS, D), 1.0, 24.0, ((0, 1024),), (0, 1, 1024, 6.0))
    weight_codes = plant(jax.random.randint(seeds[1], (D, KV), -127, 128), jax.random.fold_in(seeds[1], 1), -127, 127).astype(jnp.int32)
    weight_scales = jnp.clip(jnp.exp(math.log(0.0006) - 1.7917595 * jax.random.uniform(seeds[2], (D // BLOCK, KV), jnp.float32) ** block_levels(seeds[2], (D // BLOCK, KV), ((0, 8),), -0.2, 0.2)), 0.0001, 0.0006)
    grad_codes = plant(jax.random.randint(seeds[3], (TOKENS, KV), -8, 8), jax.random.fold_in(seeds[3], 1), -8, 7).astype(jnp.int32)
    grad_scales = jnp.clip(jnp.exp(math.log(0.5) - 2.3025851 * jax.random.uniform(seeds[4], (TOKENS, HEADS_KV), jnp.float32) ** block_levels(seeds[4], (TOKENS, HEADS_KV), ((0, 1024),), -0.2, 0.2)), 0.05, 0.5)
    return {"tokens": tokens, "weight_codes": weight_codes, "weight_scales": weight_scales, "grad_codes": grad_codes, "grad_scales": grad_scales}


def dequant_weight(weight_codes, weight_scales):
    blocks = weight_codes.astype(jnp.float32).reshape(D // BLOCK, BLOCK, KV)
    return (blocks * weight_scales[:, None, :]).reshape(D, KV).astype(jnp.bfloat16)

def decode_grad(grad_codes, grad_scales):
    coded = grad_codes.astype(jnp.float32).reshape(TOKENS, HEADS_KV, HEAD_DIM)
    return (coded * grad_scales[:, :, None]).reshape(TOKENS, KV).astype(jnp.bfloat16)

def reference(tokens, weight_codes, weight_scales, grad_codes, grad_scales):
    weight = dequant_weight(weight_codes, weight_scales)
    upstream = decode_grad(grad_codes, grad_scales)
    values = jnp.dot(tokens, weight, preferred_element_type=jnp.float32).astype(jnp.bfloat16)
    tokens_grad = lax.dot_general(upstream, weight, (((1,), (1,)), ((), ())), preferred_element_type=jnp.float32).astype(jnp.bfloat16)
    device_total = N_HST * N_OUTER
    token_blocks = tokens.reshape(device_total, TOK_DEV, D)
    grad_blocks = upstream.reshape(device_total, TOK_DEV, KV)

    def accumulate(total, pair):
        token_part, grad_part = pair
        term = lax.dot_general(token_part, grad_part, (((0,), (0,)), ((), ())), preferred_element_type=jnp.float32)
        rounded = lax.optimization_barrier(term.astype(jnp.bfloat16))
        return (total + rounded.astype(jnp.float32), None)
    weight_grad, unused = lax.scan(accumulate, jnp.zeros((D, KV), jnp.float32), (token_blocks, grad_blocks))
    return (values, tokens_grad, weight_grad)
```

```python
import jax
import jax.numpy as jnp
from jax import lax
from jax.experimental import pallas as pl
from jax.experimental.pallas import tpu as pltpu
from jax.sharding import PartitionSpec as P

F32, BF16 = jnp.float32, jnp.bfloat16
NX, NY, NZ = 4, 8, 16
LO = 4
TOK, D, KV, ROWS, HEADS = 128, 4096, 512, 512, 4
HALF = ROWS // 2
FIRST = (256, 512, 768, 896)
COUNT = (128, 128, 64, 64)


def kernel(
    tok_hbm, wc_hbm, ws_ref, gc_hbm, gs_ref,
    val_ref, tg_ref, wg_ref,
    tok, wc, gc, wbuf, trecv, urecv, vacc, term, xsend, xown, xrecv, ysend, yrecv, zsend, zrecv,
    in_sem, tsend, trcv, ownsem, usend, urcv, ucsend, ucrcv,
    wsend, wrcv, wcsend, wcrcv, xs_sem, xr_sem, ys_sem, yr_sem, zs_sem, zr_sem,
):
    h, o = lax.axis_index("hst"), lax.axis_index("outer")
    c, ylo = lax.rem(h, 2), h // 2
    yhi, x, z = lax.rem(o, 2), lax.rem(o // 2, NX), o // (2 * NX)
    y = yhi * LO + ylo
    oc = 1 - c

    def dev(x, y, z, c):
        return (lax.rem(y, LO) * 2 + c, (z * NX + x) * 2 + y // LO)

    def at_z(step):
        return lax.rem(z + step + NZ, NZ)

    def at_y(step):
        return lax.rem(y + step + NY, NY)

    def at_x(step):
        return lax.rem(x + step, NX)

    def pair_of(y):
        return (y // LO) * LO + lax.rem(2 * lax.rem(y, LO) + 1, 5)

    def unpair(p):
        return (p // LO) * LO + lax.rem(3 * lax.rem(p, LO) + 2, 5)

    def remote(src, dst, ssem, rsem, to):
        return pltpu.make_async_remote_copy(
            src_ref=src, dst_ref=dst, send_sem=ssem, recv_sem=rsem,
            device_id=to, device_id_type=pl.DeviceIdType.MESH,
        )

    pair = pair_of(y)
    finals = [
        dev(x, g * LO + lax.rem(z, LO), 2 * pair + b, c) for b in range(2) for g in range(2)
    ]
    sources = [dev(x, unpair(z // 2), ylo + LO * g, c) for g in range(4)]
    zsteps = (1, -1, 2, -2)

    load_tok = pltpu.make_async_copy(tok_hbm, tok, in_sem.at[0])
    load_wc = pltpu.make_async_copy(wc_hbm, wc, in_sem.at[1])
    load_gc = pltpu.make_async_copy(gc_hbm, gc, in_sem.at[2])
    load_gc.start()
    load_wc.start()
    load_tok.start()

    barrier = pltpu.get_barrier_semaphore()
    partners = [dev(x, y, z, oc)]
    partners += [dev(x, at_y(s), z, c) for s in range(1, NY)]
    partners += [dev(x, y, at_z(s), cc) for s in zsteps for cc in (c, oc)]
    partners += [dev(at_x(s), y, z, c) for s in range(1, NX)]
    partners += finals + sources
    for p in partners:
        pl.semaphore_signal(barrier, inc=1, device_id=p, device_id_type=pl.DeviceIdType.MESH)
    pl.semaphore_wait(barrier, len(partners))

    def columns(zz, cc):
        return pl.ds(pl.multiple_of((lax.rem(zz, LO) * 2 + cc) * ROWS, ROWS), ROWS)

    own_tok = pltpu.make_async_copy(
        tok_hbm.at[:, columns(z, c)], trecv.at[pl.ds(0, TOK)], ownsem
    )
    own_tok.start()
    other_tok = remote(
        tok_hbm.at[:, columns(z, oc)], trecv.at[pl.ds(TOK, TOK)], tsend.at[8], trcv.at[8],
        dev(x, y, z, oc),
    )
    other_tok.start()
    tok_copies = []
    for i, s in enumerate(zsteps):
        first = 64 if s == -2 else 0
        for j, cc in enumerate((c, oc)):
            copy = remote(
                tok_hbm.at[pl.ds(first, COUNT[i]), columns(at_z(s), cc)],
                trecv.at[pl.ds(FIRST[i] + j * COUNT[i], COUNT[i])],
                tsend.at[2 * i + j], trcv.at[2 * i + j], dev(x, y, at_z(s), cc),
            )
            tok_copies.append(copy)

    load_gc.wait()
    for k in range(HEADS):
        lanes = slice(k * 128, (k + 1) * 128)
        urecv[0:TOK, lanes] = (gc[:, lanes].astype(F32) * gs_ref[:, k : k + 1]).astype(BF16)
    other_up = remote(
        urecv.at[pl.ds(0, TOK)], urecv.at[pl.ds(TOK, TOK)], ucsend.at[4], ucrcv.at[4],
        dev(x, y, z, oc),
    )
    other_up.start()
    up_copies = []
    for i, s in enumerate(zsteps):
        first = 64 if s == -2 else 0
        copy = remote(
            urecv.at[pl.ds(first, COUNT[i])], urecv.at[pl.ds(FIRST[i], COUNT[i])],
            usend.at[i], urcv.at[i], dev(x, y, at_z(s), c),
        )
        copy.start()
        up_copies.append(copy)
    for copy in tok_copies:
        copy.start()

    load_wc.wait()
    for b in range(ROWS // 128):
        rows = slice(b * 128, (b + 1) * 128)
        wbuf[h, rows, :] = (wc[rows, :].astype(F32) * ws_ref[b : b + 1, :]).astype(BF16)

    def part(ylo_of, cc, half):
        return wbuf.at[ylo_of * 2 + cc, pl.ds(half * HALF, HALF)]

    left, right, far = lax.rem(ylo + 3, LO), lax.rem(ylo + 1, LO), lax.rem(ylo + 2, LO)
    to_left, to_right, to_core = dev(x, at_y(-1), z, c), dev(x, at_y(1), z, c), dev(x, y, z, oc)
    w_copies = []

    def send_w(which, half, ssem, rsem, to):
        src = part(which, c, half)
        copy = remote(src, src, ssem, rsem, to)
        copy.start()
        w_copies.append(copy)
        return copy

    send_w(ylo, 0, wsend.at[0], wrcv.at[0], to_right)
    send_w(ylo, 1, wsend.at[3], wrcv.at[3], to_left)
    send_w(ylo, 1, wsend.at[1], wrcv.at[1], to_right)
    send_w(ylo, 0, wsend.at[2], wrcv.at[2], to_left)
    send_w(ylo, 0, wcsend.at[6], wcrcv.at[6], to_core)
    send_w(ylo, 1, wcsend.at[7], wcrcv.at[7], to_core)
    where = ((left, 0), (left, 1), (right, 0), (right, 1), (far, 0), (far, 1), (ylo, 0), (ylo, 1))

    def arrived(i):
        which, half = where[i]
        ref = part(which, c, half)
        remote(ref, ref, wsend.at[i], wrcv.at[i], to_core).wait_recv()

    def arrived_core(i):
        which, half = where[i]
        ref = part(which, oc, half)
        remote(ref, ref, wcsend.at[i], wcrcv.at[i], to_core).wait_recv()

    def pass_on(i):
        which, half = where[i]
        send_w(which, half, wcsend.at[i], wcrcv.at[i], to_core)

    load_tok.wait()
    vacc[...] = jnp.zeros_like(vacc)

    def multiply(i, cc):
        which, half = where[i]
        slot = which * 2 + cc
        lanes = pl.ds(pl.multiple_of(slot * ROWS + half * HALF, HALF), HALF)
        piece = wbuf[slot, half * HALF : (half + 1) * HALF, :]
        vacc[...] += jnp.dot(tok[:, lanes], piece, preferred_element_type=F32)
        tg_ref[:, lanes] = lax.dot_general(
            urecv[0:TOK, :], piece, (((1,), (1,)), ((), ())), preferred_element_type=F32
        ).astype(BF16)

    def add_term(first, fresh):
        @pl.loop(0, 2)
        def _(m):
            lanes = pl.ds(pl.multiple_of(m * 256, 256), 256)
            product = lax.dot_general(
                trecv[first : first + 256, lanes], urecv[first : first + 256, :],
                (((0,), (0,)), ((), ())), preferred_element_type=F32,
            )
            if fresh:
                term[lanes, :] = product
            else:
                term[lanes, :] += product

    multiply(6, c)
    multiply(7, c)
    arrived(0)
    send_w(left, 0, wsend.at[4], wrcv.at[4], to_right)
    pass_on(0)
    arrived(3)
    send_w(right, 1, wsend.at[5], wrcv.at[5], to_left)
    pass_on(3)

    for i in range(4):
        up_copies[i].wait_recv()
        rows = urecv.at[pl.ds(FIRST[i], COUNT[i])]
        copy = remote(
            rows, urecv.at[pl.ds(FIRST[i] + COUNT[i], COUNT[i])], ucsend.at[i], ucrcv.at[i], to_core
        )
        copy.start()
        up_copies.append(copy)

    own_tok.wait()
    other_tok.wait_recv()
    other_up.wait_recv()
    add_term(0, True)
    arrived_core(6)
    multiply(6, oc)
    arrived_core(7)
    multiply(7, oc)
    multiply(0, c)
    multiply(3, c)
    arrived(1)
    pass_on(1)
    arrived(2)
    pass_on(2)
    multiply(1, c)
    multiply(2, c)
    arrived_core(0)
    multiply(0, oc)
    arrived_core(3)
    multiply(3, oc)

    def neighbours(i):
        tok_copies[2 * i].wait_recv()
        tok_copies[2 * i + 1].wait_recv()
        up_copies[4 + i].wait_recv()

    neighbours(0)
    add_term(FIRST[0], False)
    neighbours(1)
    add_term(FIRST[1], False)
    arrived(4)
    pass_on(4)
    arrived(5)
    pass_on(5)
    neighbours(2)
    neighbours(3)
    add_term(FIRST[2], False)

    def of_x(xx):
        rows = [
            term[pl.ds(pl.multiple_of(a * 32 + xx * 8, 8), 8), :] for a in range(NZ)
        ]
        return jnp.concatenate(rows, axis=0)

    x_copies = []
    for s in (2, 1, 3):
        xsend[s - 1] = of_x(at_x(s)).astype(BF16)
        copy = remote(
            xsend.at[s - 1], xrecv.at[s - 1], xs_sem.at[s - 1], xr_sem.at[s - 1],
            dev(at_x(s), y, z, c),
        )
        copy.start()
        x_copies.append(copy)
    xown[...] = of_x(x)

    arrived_core(1)
    multiply(1, oc)
    arrived_core(2)
    multiply(2, oc)
    multiply(4, c)
    multiply(5, c)

    for copy in x_copies:
        copy.wait_recv()
    total = xown[...]
    for s in range(NX - 1):
        total += xrecv[s].astype(F32)
    for p in range(NY):
        ysend[p] = total[p * 16 : (p + 1) * 16, :].astype(BF16)
    y_copies = []
    for s in (4, 3, 5, 2, 6, 1, 7):
        copy = remote(
            ysend.at[pair_of(at_y(s))], yrecv.at[s - 1], ys_sem.at[s - 1], yr_sem.at[s - 1],
            dev(x, at_y(s), z, c),
        )
        copy.start()
        y_copies.append(copy)

    arrived_core(4)
    multiply(4, oc)
    arrived_core(5)
    multiply(5, oc)
    val_ref[...] = vacc[...].astype(BF16)

    for copy in y_copies:
        copy.wait_recv()
    total = ysend[pair].astype(F32)
    for s in range(NY - 1):
        total += yrecv[s].astype(F32)
    zsend[0] = total[0:8, :]
    zsend[1] = total[8:16, :]
    z_copies = []
    for i, to in enumerate(finals):
        copy = remote(
            zsend.at[i // 2], zrecv.at[z // LO], zs_sem.at[i], zr_sem.at[z // LO], to
        )
        copy.start()
        z_copies.append(copy)
    for g in range(4):
        remote(zsend.at[0], zrecv.at[g], zs_sem.at[g], zr_sem.at[g], to_core).wait_recv()
    final = (zrecv[0] + zrecv[1]) + (zrecv[2] + zrecv[3])
    wg_ref[...] = jnp.where(yhi == 0, final[0:4, :], final[4:8, :])

    other_tok.wait_send()
    other_up.wait_send()
    for copy in tok_copies + up_copies + w_copies + x_copies + y_copies + z_copies:
        copy.wait_send()


def body(tokens, weight_codes, weight_scales, grad_codes, grad_scales):
    any_space = pl.BlockSpec(memory_space=pl.ANY)
    vmem = pl.BlockSpec(memory_space=pltpu.VMEM)
    dma = pltpu.SemaphoreType.DMA
    return pl.pallas_call(
        kernel,
        out_shape=(
            jax.ShapeDtypeStruct((TOK, KV), BF16),
            jax.ShapeDtypeStruct((TOK, D), BF16),
            jax.ShapeDtypeStruct((4, KV), F32),
        ),
        in_specs=[any_space, any_space, vmem, any_space, vmem],
        out_specs=(vmem, vmem, vmem),
        scratch_shapes=[
            pltpu.VMEM((TOK, D), BF16),
            pltpu.VMEM((ROWS, KV), jnp.int32),
            pltpu.VMEM((TOK, KV), jnp.int32),
            pltpu.VMEM((8, ROWS, KV), BF16),
            pltpu.VMEM((1024, ROWS), BF16),
            pltpu.VMEM((1024, KV), BF16),
            pltpu.VMEM((TOK, KV), F32),
            pltpu.VMEM((ROWS, KV), F32),
            pltpu.VMEM((NX - 1, 128, KV), BF16),
            pltpu.VMEM((128, KV), F32),
            pltpu.VMEM((NX - 1, 128, KV), BF16),
            pltpu.VMEM((NY, 16, KV), BF16),
            pltpu.VMEM((NY - 1, 16, KV), BF16),
            pltpu.VMEM((2, 8, KV), F32),
            pltpu.VMEM((4, 8, KV), F32),
            dma((3,)),
            dma((9,)), dma((9,)), dma,
            dma((4,)), dma((4,)), dma((5,)), dma((5,)),
            dma((6,)), dma((6,)), dma((8,)), dma((8,)),
            dma((3,)), dma((3,)), dma((7,)), dma((7,)), dma((4,)), dma((4,)),
        ],
        compiler_params=pltpu.CompilerParams(
            collective_id=0, has_side_effects=True, vmem_limit_bytes=40 * 1024 * 1024
        ),
    )(tokens, weight_codes, weight_scales, grad_codes, grad_scales)


def solution(mesh):
    return jax.shard_map(
        body,
        mesh=mesh,
        in_specs=(
            P(("hst", "outer"), None),
            P("hst", None),
            P("hst", None),
            P(("hst", "outer"), None),
            P(("hst", "outer"), None),
        ),
        out_specs=(P(("hst", "outer"), None), P(("hst", "outer"), None), P(("hst", "outer"), None)),
        check_vma=False,
    )
```

```python
import jax
import jax.numpy as jnp
from jax import lax
from jax.experimental import pallas as pl
from jax.experimental.pallas import tpu as pltpu
from jax.sharding import PartitionSpec as P

F32, BF16 = jnp.float32, jnp.bfloat16
NX, NY, NZ = 4, 8, 16
LO = 4
TOK, D, KV, ROWS, HEADS = 128, 4096, 512, 512, 4
HALF = ROWS // 2
XSTEPS, XFIRST, XCOUNT = (1, 3, 2), (256, 512, 768), (128, 128, 128)
ZSTEPS, ZFIRST, ZCOUNT = (1, -1, 2, -2), (256, 512, 768, 896), (128, 128, 64, 64)


def kernel(
    tok_hbm, wc_hbm, ws_ref, gc_hbm, gs_ref,
    val_hbm, tg_hbm, wg_ref,
    val_ref, tg_ref, tok, wc, gc, wbuf, tx, tz, ux, uz, vacc, term_x, term_z,
    zout, zin, zown, xout, xin, xown, ysend, yrecv, fsend, frecv,
    in_sem, own_sem, core_tsend, core_trcv, tx_send, tx_rcv, tz_send, tz_rcv,
    ux_send, ux_rcv, uz_send, uz_rcv, uc_send, uc_rcv,
    wsend, wrcv, wcsend, wcrcv, z_send, z_rcv, x_send, x_rcv, y_send, y_rcv, f_send, f_rcv, out_sem,
):
    h, o = lax.axis_index("hst"), lax.axis_index("outer")
    c, ylo = lax.rem(h, 2), h // 2
    yhi, x, z = lax.rem(o, 2), lax.rem(o // 2, NX), o // (2 * NX)
    y = yhi * LO + ylo
    oc = 1 - c
    klass = lax.rem(z, LO)

    def dev(x, y, z, c):
        return (lax.rem(y, LO) * 2 + c, (z * NX + x) * 2 + y // LO)

    def at_z(step):
        return lax.rem(z + step + NZ, NZ)

    def at_y(step):
        return lax.rem(y + step + NY, NY)

    def at_x(step):
        return lax.rem(x + step, NX)

    def remote(src, dst, ssem, rsem, to):
        return pltpu.make_async_remote_copy(
            src_ref=src, dst_ref=dst, send_sem=ssem, recv_sem=rsem,
            device_id=to, device_id_type=pl.DeviceIdType.MESH,
        )

    def signal(to):
        pl.semaphore_signal(barrier, inc=1, device_id=to, device_id_type=pl.DeviceIdType.MESH)

    by_x = ylo < 2
    final_x = jnp.where(by_x, klass, x)
    final_q = jnp.where(by_x, x, klass)
    finals = [dev(final_x, y, final_q * LO + i, c) for i in range(LO)]
    final_self = [(final_x == x) & (final_q * LO + i == z) for i in range(LO)]
    source_x = jnp.where(by_x, z // LO, x)
    source_k = jnp.where(by_x, x, z // LO)
    sources = [dev(source_x, y, source_k + LO * g, c) for g in range(4)]
    source_self = [(source_x == x) & (source_k + LO * g == z) for g in range(4)]
    loner = (final_x == x) & (final_q == z // LO)

    load_tok = pltpu.make_async_copy(tok_hbm, tok, in_sem.at[0])
    load_wc = pltpu.make_async_copy(wc_hbm, wc, in_sem.at[1])
    load_gc = pltpu.make_async_copy(gc_hbm, gc, in_sem.at[2])
    load_gc.start()
    load_wc.start()
    load_tok.start()

    def columns(ylo_of, cc, q):
        return pl.ds(pl.multiple_of(((ylo_of * 2 + cc) * 4 + q) * 128, 128), 128)

    own_copies = []
    for j in range(2):
        lanes = pl.ds(j * 128, 128)
        own_copies.append(pltpu.make_async_copy(
            tok_hbm.at[:, columns(j, c, x)], tx.at[pl.ds(0, TOK), lanes], own_sem.at[j]
        ))
        own_copies.append(pltpu.make_async_copy(
            tok_hbm.at[:, columns(2 + j, c, klass)], tz.at[pl.ds(0, TOK), lanes], own_sem.at[2 + j]
        ))
    for copy in own_copies:
        copy.start()

    barrier = pltpu.get_barrier_semaphore()
    partners = [dev(x, y, z, oc)]
    partners += [dev(x, at_y(s), z, c) for s in range(1, NY)]
    partners += [dev(x, y, at_z(s), cc) for s in ZSTEPS for cc in (c, oc)]
    partners += [dev(at_x(s), y, z, cc) for s in XSTEPS for cc in (c, oc)]
    for p in partners:
        signal(p)
    for p, same in zip(finals + sources, final_self + source_self):
        @pl.when(jnp.logical_not(same))
        def _(p=p):
            signal(p)
    pl.semaphore_wait(barrier, jnp.where(loner, len(partners) + 6, len(partners) + 8))

    core_copies, tx_copies, tz_copies = [], [], []
    for j in range(2):
        lanes = pl.ds(j * 128, 128)
        core_copies.append(remote(
            tok_hbm.at[:, columns(j, oc, x)], tx.at[pl.ds(TOK, TOK), lanes],
            core_tsend.at[j], core_trcv.at[j], dev(x, y, z, oc),
        ))
        core_copies.append(remote(
            tok_hbm.at[:, columns(2 + j, oc, klass)], tz.at[pl.ds(TOK, TOK), lanes],
            core_tsend.at[2 + j], core_trcv.at[2 + j], dev(x, y, z, oc),
        ))
    for i, s in enumerate(XSTEPS):
        for k, cc in enumerate((c, oc)):
            for j in range(2):
                tx_copies.append(remote(
                    tok_hbm.at[:, columns(j, cc, at_x(s))],
                    tx.at[pl.ds(XFIRST[i] + k * XCOUNT[i], XCOUNT[i]), pl.ds(j * 128, 128)],
                    tx_send.at[4 * i + 2 * k + j], tx_rcv.at[4 * i + 2 * k + j],
                    dev(at_x(s), y, z, cc),
                ))
    for i, s in enumerate(ZSTEPS):
        first = 64 if s == -2 else 0
        for k, cc in enumerate((c, oc)):
            for j in range(2):
                tz_copies.append(remote(
                    tok_hbm.at[pl.ds(first, ZCOUNT[i]), columns(2 + j, cc, lax.rem(at_z(s), LO))],
                    tz.at[pl.ds(ZFIRST[i] + k * ZCOUNT[i], ZCOUNT[i]), pl.ds(j * 128, 128)],
                    tz_send.at[4 * i + 2 * k + j], tz_rcv.at[4 * i + 2 * k + j],
                    dev(x, y, at_z(s), cc),
                ))
    for copy in tx_copies[8:] + tz_copies[8:] + core_copies:
        copy.start()

    load_gc.wait()
    scales = gs_ref[...].T
    for k in range(HEADS):
        lanes = slice(k * 128, (k + 1) * 128)
        ux[0:TOK, lanes] = (gc[:, lanes].astype(F32) * scales[:, k : k + 1]).astype(BF16)
    to_core = dev(x, y, z, oc)
    up_own = remote(
        ux.at[pl.ds(0, TOK)], ux.at[pl.ds(TOK, TOK)], uc_send.at[7], uc_rcv.at[7], to_core
    )
    ux_copies = [
        remote(
            ux.at[pl.ds(0, TOK)], ux.at[pl.ds(XFIRST[i], TOK)],
            ux_send.at[i], ux_rcv.at[i], dev(at_x(s), y, z, c),
        )
        for i, s in enumerate(XSTEPS)
    ]
    uz_copies = [
        remote(
            ux.at[pl.ds(64 if s == -2 else 0, ZCOUNT[i])], uz.at[pl.ds(ZFIRST[i], ZCOUNT[i])],
            uz_send.at[i], uz_rcv.at[i], dev(x, y, at_z(s), c),
        )
        for i, s in enumerate(ZSTEPS)
    ]
    for copy in ux_copies + uz_copies + [up_own]:
        copy.start()
    for copy in tx_copies[:8] + tz_copies[:8]:
        copy.start()
    uc_copies = [
        remote(
            ux.at[pl.ds(XFIRST[i], TOK)], ux.at[pl.ds(XFIRST[i] + TOK, TOK)],
            uc_send.at[i], uc_rcv.at[i], to_core,
        )
        for i in range(3)
    ] + [
        remote(
            uz.at[pl.ds(ZFIRST[i], ZCOUNT[i])], uz.at[pl.ds(ZFIRST[i] + ZCOUNT[i], ZCOUNT[i])],
            uc_send.at[3 + i], uc_rcv.at[3 + i], to_core,
        )
        for i in range(4)
    ]

    load_wc.wait()
    for b in range(ROWS // 128):
        rows = slice(b * 128, (b + 1) * 128)
        wbuf[h, rows, :] = (wc[rows, :].astype(F32) * ws_ref[b : b + 1, :]).astype(BF16)

    def part(ylo_of, cc, half):
        return wbuf.at[ylo_of * 2 + cc, pl.ds(half * HALF, HALF)]

    left, right, far = lax.rem(ylo + 3, LO), lax.rem(ylo + 1, LO), lax.rem(ylo + 2, LO)
    to_left, to_right = dev(x, at_y(-1), z, c), dev(x, at_y(1), z, c)
    w_copies = []

    def send_w(which, half, ssem, rsem, to):
        src = part(which, c, half)
        copy = remote(src, src, ssem, rsem, to)
        copy.start()
        w_copies.append(copy)

    send_w(ylo, 0, wsend.at[0], wrcv.at[0], to_right)
    send_w(ylo, 1, wsend.at[3], wrcv.at[3], to_left)
    send_w(ylo, 1, wsend.at[1], wrcv.at[1], to_right)
    send_w(ylo, 0, wsend.at[2], wrcv.at[2], to_left)
    send_w(ylo, 0, wcsend.at[6], wcrcv.at[6], to_core)
    send_w(ylo, 1, wcsend.at[7], wcrcv.at[7], to_core)
    where = ((left, 0), (left, 1), (right, 0), (right, 1), (far, 0), (far, 1), (ylo, 0), (ylo, 1))

    def arrived(i):
        which, half = where[i]
        ref = part(which, c, half)
        remote(ref, ref, wsend.at[i], wrcv.at[i], to_core).wait_recv()

    def arrived_core(i):
        which, half = where[i]
        ref = part(which, oc, half)
        remote(ref, ref, wcsend.at[i], wcrcv.at[i], to_core).wait_recv()

    def pass_on(i):
        which, half = where[i]
        send_w(which, half, wcsend.at[i], wcrcv.at[i], to_core)

    load_tok.wait()
    vacc[...] = jnp.zeros_like(vacc)

    def multiply(i, cc):
        which, half = where[i]
        slot = which * 2 + cc
        lanes = pl.ds(pl.multiple_of(slot * ROWS + half * HALF, HALF), HALF)
        piece = wbuf[slot, half * HALF : (half + 1) * HALF, :]
        vacc[...] += jnp.dot(tok[:, lanes], piece, preferred_element_type=F32)
        tg_ref[:, lanes] = lax.dot_general(
            ux[0:TOK, :], piece, (((1,), (1,)), ((), ())), preferred_element_type=F32
        ).astype(BF16)

    def product(tokens, upstream, first):
        return lax.dot_general(
            tokens[first : first + 256, :], upstream[first : first + 256, :],
            (((0,), (0,)), ((), ())), preferred_element_type=F32,
        )

    multiply(6, c)
    multiply(7, c)
    arrived(0)
    send_w(left, 0, wsend.at[4], wrcv.at[4], to_right)
    pass_on(0)
    arrived(3)
    send_w(right, 1, wsend.at[5], wrcv.at[5], to_left)
    pass_on(3)

    def up_pass_on(copy, i):
        copy.wait_recv()
        uc_copies[i].start()

    for i in (0, 1):
        up_pass_on(ux_copies[i], i)
        up_pass_on(uz_copies[i], 3 + i)

    for copy in own_copies:
        copy.wait()
    for copy in core_copies + [up_own]:
        copy.wait_recv()
    term_x[...] = product(tx, ux, 0)
    term_z[...] = product(tz, ux, 0)
    up_pass_on(ux_copies[2], 2)
    up_pass_on(uz_copies[2], 5)
    up_pass_on(uz_copies[3], 6)
    arrived_core(6)
    multiply(6, oc)
    arrived_core(7)
    multiply(7, oc)
    multiply(0, c)
    multiply(3, c)

    def wait_x(i):
        for copy in tx_copies[4 * i : 4 * i + 4] + [uc_copies[i]]:
            copy.wait_recv()

    def wait_z(i):
        for copy in tz_copies[4 * i : 4 * i + 4] + [uc_copies[3 + i]]:
            copy.wait_recv()

    for i in range(2):
        wait_x(i)
        term_x[...] += product(tx, ux, XFIRST[i])
        wait_z(i)
        term_z[...] += product(tz, uz, ZFIRST[i])

    def of_x(term, xx):
        rows = [term[pl.ds(pl.multiple_of(a * 32 + xx * 8, 8), 8), :] for a in range(8)]
        return jnp.concatenate(rows, axis=0)

    wait_x(2)
    term_x[...] += product(tx, ux, XFIRST[2])
    zout_copies = []
    for i, s in enumerate((2, 1, -1)):
        zout[i] = of_x(term_x, lax.rem(at_z(s), LO)).astype(BF16)
        if s == 2:
            pieces = ((0, 32, 2, 2, 2), (32, 32, -2, 2, 3))
        else:
            pieces = ((0, 64, s, 0 if s == 1 else 1, 0 if s == 1 else 1),)
        for first, count, step, slot, sem in pieces:
            copy = remote(
                zout.at[i, pl.ds(first, count)], zin.at[slot, pl.ds(first, count)],
                z_send.at[sem], z_rcv.at[sem], dev(x, y, at_z(step), c),
            )
            copy.start()
            zout_copies.append(copy)
    zown[...] = of_x(term_x, klass)
    wait_z(2)
    wait_z(3)
    term_z[...] += product(tz, uz, ZFIRST[2])
    xout_copies = []
    for i, s in enumerate((2, 1, 3)):
        xout[i] = of_x(term_z, at_x(s)).astype(BF16)
        copy = remote(
            xout.at[i], xin.at[i], x_send.at[i], x_rcv.at[i], dev(at_x(s), y, z, c)
        )
        copy.start()
        xout_copies.append(copy)
    xown[...] = of_x(term_z, x)

    arrived(1)
    pass_on(1)
    arrived(2)
    pass_on(2)
    multiply(1, c)
    multiply(2, c)
    arrived_core(0)
    multiply(0, oc)
    arrived_core(3)
    multiply(3, oc)

    upper = lax.broadcasted_iota(jnp.int32, (8, KV), 0) < 4

    def regroup(total, first_ylo):
        for j in range(2):
            low, high = [], []
            for k in range(2):
                row = j * 32 + k * 16
                a, b = total[row : row + 8, :], total[row + 8 : row + 16, :]
                low.append(jnp.where(upper, a, pltpu.roll(b, 4, 0)))
                high.append(jnp.where(upper, pltpu.roll(a, 4, 0), b))
            ysend[first_ylo + j] = jnp.concatenate(low, axis=0).astype(BF16)
            ysend[LO + first_ylo + j] = jnp.concatenate(high, axis=0).astype(BF16)

    for copy in zout_copies:
        copy.wait_recv()
    regroup(
        (zown[...] + zin[0].astype(F32)) + (zin[1].astype(F32) + zin[2].astype(F32)), 0
    )
    for copy in xout_copies:
        copy.wait_recv()
    regroup(
        (xown[...] + xin[0].astype(F32)) + (xin[1].astype(F32) + xin[2].astype(F32)), 2
    )
    y_copies = []
    for s in (4, 3, 5, 2, 6, 1, 7):
        copy = remote(
            ysend.at[at_y(s)], yrecv.at[s - 1], y_send.at[s - 1], y_rcv.at[s - 1],
            dev(x, at_y(s), z, c),
        )
        copy.start()
        y_copies.append(copy)

    arrived(4)
    pass_on(4)
    arrived(5)
    pass_on(5)
    multiply(4, c)
    multiply(5, c)
    arrived_core(1)
    multiply(1, oc)
    arrived_core(2)
    multiply(2, oc)

    for copy in y_copies:
        copy.wait_recv()
    total = ysend[y].astype(F32)
    for s in range(NY - 1):
        total += yrecv[s].astype(F32)
    fsend[0] = total[0:8, :]
    fsend[1] = total[8:16, :]
    f_copies = []
    for i in range(LO):
        copy = remote(
            fsend.at[i // 2], frecv.at[z // LO], f_send.at[i], f_rcv.at[z // LO], finals[i]
        )
        f_copies.append(copy)

        @pl.when(jnp.logical_not(final_self[i]))
        def _(copy=copy):
            copy.start()

        @pl.when(final_self[i])
        def _(i=i):
            frecv[z // LO] = fsend[i // 2]

    arrived_core(4)
    multiply(4, oc)
    arrived_core(5)
    multiply(5, oc)
    val_ref[...] = vacc[...].astype(BF16)
    out_copies = [
        pltpu.make_async_copy(tg_ref, tg_hbm, out_sem.at[0]),
        pltpu.make_async_copy(val_ref, val_hbm, out_sem.at[1]),
    ]
    for copy in out_copies:
        copy.start()

    for g in range(4):
        @pl.when(jnp.logical_not(source_self[g]))
        def _(g=g):
            remote(fsend.at[0], frecv.at[g], f_send.at[g], f_rcv.at[g], to_core).wait_recv()
    final = (frecv[0] + frecv[1]) + (frecv[2] + frecv[3])
    wg_ref[...] = jnp.where(lax.rem(z, 2) == 0, final[0:4, :], final[4:8, :])

    for copy in (
        core_copies + tx_copies + tz_copies + ux_copies + uz_copies + [up_own] + uc_copies
        + w_copies + zout_copies + xout_copies + y_copies
    ):
        copy.wait_send()
    for i in range(LO):
        @pl.when(jnp.logical_not(final_self[i]))
        def _(i=i):
            f_copies[i].wait_send()
    for copy in out_copies:
        copy.wait()


def writer(val_in, tg_in, wg_in, val_out, tg_out, wg_out, val, tg, wg, in_sem, out_sem):
    pieces = [(val_in, val, val_out), (wg_in, wg, wg_out)]
    for i in range(4):
        rows = pl.ds(i * (TOK // 4), TOK // 4)
        pieces.append((tg_in.at[rows], tg.at[rows], tg_out.at[rows]))
    ins = [pltpu.make_async_copy(a, b, in_sem.at[i]) for i, (a, b, _) in enumerate(pieces)]
    outs = [pltpu.make_async_copy(b, c, out_sem.at[i]) for i, (_, b, c) in enumerate(pieces)]
    for copy in ins:
        copy.start()
    for i, copy in enumerate(ins):
        copy.wait()
        outs[i].start()
    for copy in outs:
        copy.wait()


def write_out(results):
    any_space = pl.BlockSpec(memory_space=pltpu.HBM)
    return pl.pallas_call(
        writer,
        out_shape=tuple(jax.ShapeDtypeStruct(r.shape, r.dtype) for r in results),
        in_specs=[any_space] * 3,
        out_specs=(any_space,) * 3,
        scratch_shapes=[pltpu.VMEM(r.shape, r.dtype) for r in results]
        + [pltpu.SemaphoreType.DMA((6,))] * 2,
        compiler_params=pltpu.CompilerParams(vmem_limit_bytes=60 * 1024 * 1024),
    )(*results)


def body(tokens, weight_codes, weight_scales, grad_codes, grad_scales):
    any_space = pl.BlockSpec(memory_space=pltpu.HBM)
    vmem = pl.BlockSpec(memory_space=pltpu.VMEM)
    dma = pltpu.SemaphoreType.DMA
    results = pl.pallas_call(
        kernel,
        out_shape=(
            jax.ShapeDtypeStruct((TOK, KV), BF16),
            jax.ShapeDtypeStruct((TOK, D), BF16),
            jax.ShapeDtypeStruct((4, KV), F32),
        ),
        in_specs=[any_space, any_space, vmem, any_space, vmem],
        out_specs=(any_space, any_space, vmem),
        scratch_shapes=[
            pltpu.VMEM((TOK, KV), BF16),
            pltpu.VMEM((TOK, D), BF16),
            pltpu.VMEM((TOK, D), BF16),
            pltpu.VMEM((ROWS, KV), jnp.int32),
            pltpu.VMEM((TOK, KV), jnp.int32),
            pltpu.VMEM((8, ROWS, KV), BF16),
            pltpu.VMEM((1024, 256), BF16),
            pltpu.VMEM((1024, 256), BF16),
            pltpu.VMEM((1024, KV), BF16),
            pltpu.VMEM((1024, KV), BF16),
            pltpu.VMEM((TOK, KV), F32),
            pltpu.VMEM((256, KV), F32),
            pltpu.VMEM((256, KV), F32),
            pltpu.VMEM((3, 64, KV), BF16),
            pltpu.VMEM((3, 64, KV), BF16),
            pltpu.VMEM((64, KV), F32),
            pltpu.VMEM((3, 64, KV), BF16),
            pltpu.VMEM((3, 64, KV), BF16),
            pltpu.VMEM((64, KV), F32),
            pltpu.VMEM((NY, 16, KV), BF16),
            pltpu.VMEM((NY - 1, 16, KV), BF16),
            pltpu.VMEM((2, 8, KV), F32),
            pltpu.VMEM((4, 8, KV), F32),
        ]
        + [
            dma((n,))
            for n in (3, 4, 4, 4, 12, 12, 16, 16, 3, 3, 4, 4, 8, 8, 6, 6, 8, 8, 4, 4, 3, 3, 7, 7, 4, 4, 2)
        ],
        compiler_params=pltpu.CompilerParams(
            collective_id=0, has_side_effects=True, vmem_limit_bytes=60 * 1024 * 1024
        ),
    )(tokens, weight_codes, weight_scales, grad_codes, grad_scales.T)
    return write_out(results)


def solution(mesh):
    return jax.shard_map(
        body,
        mesh=mesh,
        in_specs=(
            P(("hst", "outer"), None),
            P("hst", None),
            P("hst", None),
            P(("hst", "outer"), None),
            P(("hst", "outer"), None),
        ),
        out_specs=(P(("hst", "outer"), None), P(("hst", "outer"), None), P(("hst", "outer"), None)),
        check_vma=False,
    )
```

```python
import jax
import jax.numpy as jnp
from jax import lax
from jax.experimental import pallas as pl
from jax.experimental.pallas import tpu as pltpu
from jax.sharding import PartitionSpec as P

F32, BF16 = jnp.float32, jnp.bfloat16
NX, NY, NZ = 4, 8, 16
LO = 4
TOK, D, KV, ROWS, HEADS = 128, 4096, 512, 512, 4
HALF = ROWS // 2
XSTEPS, XFIRST, XCOUNT = (1, 3, 2), (256, 512, 768), (128, 128, 128)
ZSTEPS, ZFIRST, ZCOUNT = (1, -1, 2, -2), (256, 512, 768, 896), (128, 128, 64, 64)


def kernel(
    tok_hbm, wc_hbm, ws_ref, gc_hbm, gs_ref,
    val_hbm, tg_hbm, frecv,
    val_ref, tg_ref, tok, wc, gc, wbuf, tx, tz, ux, uz, vacc, term_x, term_z,
    zout, zin, zown, xout, xin, xown, ysend, yrecv, fsend,
    in_sem, own_sem, core_tsend, core_trcv, tx_send, tx_rcv, tz_send, tz_rcv,
    ux_send, ux_rcv, uz_send, uz_rcv, uc_send, uc_rcv,
    wsend, wrcv, wcsend, wcrcv, z_send, z_rcv, x_send, x_rcv, y_send, y_rcv, f_send, f_rcv, out_sem,
):
    h, o = lax.axis_index("hst"), lax.axis_index("outer")
    c, ylo = lax.rem(h, 2), h // 2
    yhi, x, z = lax.rem(o, 2), lax.rem(o // 2, NX), o // (2 * NX)
    y = yhi * LO + ylo
    oc = 1 - c
    klass = lax.rem(z, LO)

    def dev(x, y, z, c):
        return (lax.rem(y, LO) * 2 + c, (z * NX + x) * 2 + y // LO)

    def at_z(step):
        return lax.rem(z + step + NZ, NZ)

    def at_y(step):
        return lax.rem(y + step + NY, NY)

    def at_x(step):
        return lax.rem(x + step, NX)

    def remote(src, dst, ssem, rsem, to):
        return pltpu.make_async_remote_copy(
            src_ref=src, dst_ref=dst, send_sem=ssem, recv_sem=rsem,
            device_id=to, device_id_type=pl.DeviceIdType.MESH,
        )

    def signal(to):
        pl.semaphore_signal(barrier, inc=1, device_id=to, device_id_type=pl.DeviceIdType.MESH)

    by_x = ylo < 2
    final_x = jnp.where(by_x, klass, x)
    final_q = jnp.where(by_x, x, klass)
    finals = [dev(final_x, y, final_q * LO + i, c) for i in range(LO)]
    final_self = [(final_x == x) & (final_q * LO + i == z) for i in range(LO)]
    source_x = jnp.where(by_x, z // LO, x)
    source_k = jnp.where(by_x, x, z // LO)
    sources = [dev(source_x, y, source_k + LO * g, c) for g in range(4)]
    source_self = [(source_x == x) & (source_k + LO * g == z) for g in range(4)]
    loner = (final_x == x) & (final_q == z // LO)

    load_tok = pltpu.make_async_copy(tok_hbm, tok, in_sem.at[0])
    load_wc = pltpu.make_async_copy(wc_hbm, wc, in_sem.at[1])
    load_gc = pltpu.make_async_copy(gc_hbm, gc, in_sem.at[2])
    load_gc.start()
    load_wc.start()
    load_tok.start()

    def columns(ylo_of, cc, q):
        return pl.ds(pl.multiple_of(((ylo_of * 2 + cc) * 4 + q) * 128, 128), 128)

    own_copies = []
    for j in range(2):
        lanes = pl.ds(j * 128, 128)
        own_copies.append(pltpu.make_async_copy(
            tok_hbm.at[:, columns(j, c, x)], tx.at[pl.ds(0, TOK), lanes], own_sem.at[j]
        ))
        own_copies.append(pltpu.make_async_copy(
            tok_hbm.at[:, columns(2 + j, c, klass)], tz.at[pl.ds(0, TOK), lanes], own_sem.at[2 + j]
        ))
    for copy in own_copies:
        copy.start()

    barrier = pltpu.get_barrier_semaphore()
    partners = [dev(x, at_y(s), z, c) for s in (4, 3, 5, 2, 6, 1, 7)]
    partners += [dev(x, y, at_z(s), cc) for s in ZSTEPS for cc in (c, oc)]
    partners += [dev(at_x(s), y, z, cc) for s in (2, 1, 3) for cc in (c, oc)]
    partners += [dev(x, y, z, oc)]
    for p in partners:
        signal(p)
    for p, same in zip(finals + sources, final_self + source_self):
        @pl.when(jnp.logical_not(same))
        def _(p=p):
            signal(p)
    load_gc.wait()
    scales = gs_ref[...].T
    for k in range(HEADS):
        lanes = slice(k * 128, (k + 1) * 128)
        ux[0:TOK, lanes] = (gc[:, lanes].astype(F32) * scales[:, k : k + 1]).astype(BF16)
    pl.semaphore_wait(barrier, jnp.where(loner, len(partners) + 6, len(partners) + 8))

    core_copies, tx_copies, tz_copies = [], [], []
    for j in range(2):
        lanes = pl.ds(j * 128, 128)
        core_copies.append(remote(
            tok_hbm.at[:, columns(j, oc, x)], tx.at[pl.ds(TOK, TOK), lanes],
            core_tsend.at[j], core_trcv.at[j], dev(x, y, z, oc),
        ))
        core_copies.append(remote(
            tok_hbm.at[:, columns(2 + j, oc, klass)], tz.at[pl.ds(TOK, TOK), lanes],
            core_tsend.at[2 + j], core_trcv.at[2 + j], dev(x, y, z, oc),
        ))
    for i, s in enumerate(XSTEPS):
        for k, cc in enumerate((c, oc)):
            for j in range(2):
                tx_copies.append(remote(
                    tok_hbm.at[:, columns(j, cc, at_x(s))],
                    tx.at[pl.ds(XFIRST[i] + k * XCOUNT[i], XCOUNT[i]), pl.ds(j * 128, 128)],
                    tx_send.at[4 * i + 2 * k + j], tx_rcv.at[4 * i + 2 * k + j],
                    dev(at_x(s), y, z, cc),
                ))
    for i, s in enumerate(ZSTEPS):
        first = 64 if s == -2 else 0
        for k, cc in enumerate((c, oc)):
            for j in range(2):
                tz_copies.append(remote(
                    tok_hbm.at[pl.ds(first, ZCOUNT[i]), columns(2 + j, cc, lax.rem(at_z(s), LO))],
                    tz.at[pl.ds(ZFIRST[i] + k * ZCOUNT[i], ZCOUNT[i]), pl.ds(j * 128, 128)],
                    tz_send.at[4 * i + 2 * k + j], tz_rcv.at[4 * i + 2 * k + j],
                    dev(x, y, at_z(s), cc),
                ))

    to_core = dev(x, y, z, oc)
    up_own = remote(
        ux.at[pl.ds(0, TOK)], ux.at[pl.ds(TOK, TOK)], uc_send.at[7], uc_rcv.at[7], to_core
    )
    ux_copies, uz_copies = [], []
    for i, s in enumerate((1, 3)):
        ux_copies.append(remote(
            ux.at[pl.ds(0, TOK)], ux.at[pl.ds(XFIRST[i], TOK)],
            ux_send.at[i], ux_rcv.at[i], dev(at_x(s), y, z, c),
        ))
    for i, s in enumerate((1, -1)):
        uz_copies.append(remote(
            ux.at[pl.ds(0, TOK)], uz.at[pl.ds(ZFIRST[i], TOK)],
            uz_send.at[i], uz_rcv.at[i], dev(x, y, at_z(s), c),
        ))
    for i, s in enumerate((1, 3)):
        ux_copies.append(remote(
            ux.at[pl.ds(XFIRST[i] + 64 * i, 64)], ux.at[pl.ds(XFIRST[2] + 64 * i, 64)],
            ux_send.at[2 + i], ux_rcv.at[2 + i], dev(at_x(s), y, z, c),
        ))
    for i, s in enumerate((1, -1)):
        uz_copies.append(remote(
            uz.at[pl.ds(ZFIRST[i] + 64 * i, 64)], uz.at[pl.ds(ZFIRST[2 + i], 64)],
            uz_send.at[2 + i], uz_rcv.at[2 + i], dev(x, y, at_z(s), c),
        ))
    for copy in ux_copies[:2] + uz_copies[:2] + [up_own]:
        copy.start()
    for copy in tx_copies[8:] + tz_copies[8:] + core_copies + tx_copies[:8] + tz_copies[:8]:
        copy.start()
    uc_copies = [
        remote(
            ux.at[pl.ds(XFIRST[i], TOK)], ux.at[pl.ds(XFIRST[i] + TOK, TOK)],
            uc_send.at[i], uc_rcv.at[i], to_core,
        )
        for i in range(3)
    ] + [
        remote(
            uz.at[pl.ds(ZFIRST[i], ZCOUNT[i])], uz.at[pl.ds(ZFIRST[i] + ZCOUNT[i], ZCOUNT[i])],
            uc_send.at[3 + i], uc_rcv.at[3 + i], to_core,
        )
        for i in range(4)
    ]


    load_wc.wait()
    for b in range(ROWS // 128):
        rows = slice(b * 128, (b + 1) * 128)
        wbuf[h, rows, :] = (wc[rows, :].astype(F32) * ws_ref[b : b + 1, :]).astype(BF16)

    def part(ylo_of, cc, half):
        return wbuf.at[ylo_of * 2 + cc, pl.ds(half * HALF, HALF)]

    left, right, far = lax.rem(ylo + 3, LO), lax.rem(ylo + 1, LO), lax.rem(ylo + 2, LO)
    to_left, to_right = dev(x, at_y(-1), z, c), dev(x, at_y(1), z, c)
    w_copies = []

    def send_w(which, half, ssem, rsem, to):
        src = part(which, c, half)
        copy = remote(src, src, ssem, rsem, to)
        copy.start()
        w_copies.append(copy)

    send_w(ylo, 0, wsend.at[0], wrcv.at[0], to_right)
    send_w(ylo, 1, wsend.at[3], wrcv.at[3], to_left)
    send_w(ylo, 1, wsend.at[1], wrcv.at[1], to_right)
    send_w(ylo, 0, wsend.at[2], wrcv.at[2], to_left)
    send_w(ylo, 0, wcsend.at[6], wcrcv.at[6], to_core)
    send_w(ylo, 1, wcsend.at[7], wcrcv.at[7], to_core)
    where = ((left, 0), (left, 1), (right, 0), (right, 1), (far, 0), (far, 1), (ylo, 0), (ylo, 1))

    def arrived(i):
        which, half = where[i]
        ref = part(which, c, half)
        remote(ref, ref, wsend.at[i], wrcv.at[i], to_core).wait_recv()

    def arrived_core(i):
        which, half = where[i]
        ref = part(which, oc, half)
        remote(ref, ref, wcsend.at[i], wcrcv.at[i], to_core).wait_recv()

    def pass_on(i):
        which, half = where[i]
        send_w(which, half, wcsend.at[i], wcrcv.at[i], to_core)

    load_tok.wait()
    vacc[...] = jnp.zeros_like(vacc)

    def multiply(i, cc):
        which, half = where[i]
        slot = which * 2 + cc
        lanes = pl.ds(pl.multiple_of(slot * ROWS + half * HALF, HALF), HALF)
        piece = wbuf[slot, half * HALF : (half + 1) * HALF, :]
        vacc[...] += jnp.dot(tok[:, lanes], piece, preferred_element_type=F32)
        tg_ref[:, lanes] = lax.dot_general(
            ux[0:TOK, :], piece, (((1,), (1,)), ((), ())), preferred_element_type=F32
        ).astype(BF16)

    def product(tokens, upstream, first):
        return lax.dot_general(
            tokens[first : first + 256, :], upstream[first : first + 256, :],
            (((0,), (0,)), ((), ())), preferred_element_type=F32,
        )

    def up_pass_on(copy, i):
        copy.wait_recv()
        uc_copies[i].start()

    for i in (0, 1):
        ux_copies[i].wait_recv()
        ux_copies[2 + i].start()
        uc_copies[i].start()
        uz_copies[i].wait_recv()
        uz_copies[2 + i].start()
        uc_copies[3 + i].start()

    arrived(0)
    send_w(left, 0, wsend.at[4], wrcv.at[4], to_right)
    pass_on(0)
    arrived(3)
    send_w(right, 1, wsend.at[5], wrcv.at[5], to_left)
    pass_on(3)
    multiply(6, c)
    multiply(7, c)
    for copy in own_copies:
        copy.wait()
    for copy in core_copies + [up_own]:
        copy.wait_recv()
    term_x[...] = product(tx, ux, 0)
    term_z[...] = product(tz, ux, 0)
    ux_copies[2].wait_recv()
    up_pass_on(ux_copies[3], 2)
    up_pass_on(uz_copies[2], 5)
    up_pass_on(uz_copies[3], 6)
    arrived_core(6)
    multiply(6, oc)
    arrived_core(7)
    multiply(7, oc)
    multiply(0, c)
    multiply(3, c)

    def wait_x(i):
        for copy in tx_copies[4 * i : 4 * i + 4] + [uc_copies[i]]:
            copy.wait_recv()

    def wait_z(i):
        for copy in tz_copies[4 * i : 4 * i + 4] + [uc_copies[3 + i]]:
            copy.wait_recv()

    for i in range(2):
        wait_x(i)
        term_x[...] += product(tx, ux, XFIRST[i])
        wait_z(i)
        term_z[...] += product(tz, uz, ZFIRST[i])

    def of_x(term, xx):
        rows = [term[pl.ds(pl.multiple_of(a * 32 + xx * 8, 8), 8), :] for a in range(8)]
        return jnp.concatenate(rows, axis=0)

    wait_x(2)
    term_x[...] += product(tx, ux, XFIRST[2])
    zout_copies = []
    for i, s in enumerate((2, 1, -1)):
        zout[i] = of_x(term_x, lax.rem(at_z(s), LO)).astype(BF16)
        if s == 2:
            pieces = ((0, 32, 2, 2, 2), (32, 32, -2, 2, 3))
        else:
            pieces = ((0, 64, s, 0 if s == 1 else 1, 0 if s == 1 else 1),)
        for first, count, step, slot, sem in pieces:
            copy = remote(
                zout.at[i, pl.ds(first, count)], zin.at[slot, pl.ds(first, count)],
                z_send.at[sem], z_rcv.at[sem], dev(x, y, at_z(step), c),
            )
            copy.start()
            zout_copies.append(copy)
    zown[...] = of_x(term_x, klass)
    wait_z(2)
    wait_z(3)
    term_z[...] += product(tz, uz, ZFIRST[2])
    xout_copies = []
    for i, s in enumerate((2, 1, 3)):
        xout[i] = of_x(term_z, at_x(s)).astype(BF16)
        copy = remote(
            xout.at[i], xin.at[i], x_send.at[i], x_rcv.at[i], dev(at_x(s), y, z, c)
        )
        copy.start()
        xout_copies.append(copy)
    xown[...] = of_x(term_z, x)

    arrived(1)
    pass_on(1)
    arrived(2)
    pass_on(2)
    multiply(1, c)
    multiply(2, c)
    arrived_core(0)
    multiply(0, oc)
    arrived_core(3)
    multiply(3, oc)

    upper = lax.broadcasted_iota(jnp.int32, (8, KV), 0) < 4

    def regroup(total, first_ylo):
        for j in range(2):
            low, high = [], []
            for k in range(2):
                row = j * 32 + k * 16
                a, b = total[row : row + 8, :], total[row + 8 : row + 16, :]
                low.append(jnp.where(upper, a, pltpu.roll(b, 4, 0)))
                high.append(jnp.where(upper, pltpu.roll(a, 4, 0), b))
            ysend[first_ylo + j] = jnp.concatenate(low, axis=0).astype(BF16)
            ysend[LO + first_ylo + j] = jnp.concatenate(high, axis=0).astype(BF16)

    for copy in zout_copies:
        copy.wait_recv()
    regroup(
        (zown[...] + zin[0].astype(F32)) + (zin[1].astype(F32) + zin[2].astype(F32)), 0
    )
    for copy in xout_copies:
        copy.wait_recv()
    regroup(
        (xown[...] + xin[0].astype(F32)) + (xin[1].astype(F32) + xin[2].astype(F32)), 2
    )
    y_copies = []
    for s in (4, 3, 5, 2, 6, 1, 7):
        copy = remote(
            ysend.at[at_y(s)], yrecv.at[s - 1], y_send.at[s - 1], y_rcv.at[s - 1],
            dev(x, at_y(s), z, c),
        )
        copy.start()
        y_copies.append(copy)

    arrived(4)
    pass_on(4)
    arrived(5)
    pass_on(5)
    multiply(4, c)
    multiply(5, c)
    arrived_core(1)
    multiply(1, oc)
    arrived_core(2)
    multiply(2, oc)

    for copy in y_copies:
        copy.wait_recv()
    total = ysend[y].astype(F32)
    for s in range(NY - 1):
        total += yrecv[s].astype(F32)
    narrow = lax.broadcasted_iota(jnp.int32, (8, 128), 0) < 4
    for b in range(2):
        t = [total[8 * b : 8 * b + 8, 128 * j : 128 * j + 128] for j in range(4)]
        r = [pltpu.roll(a, 4, 0) for a in t]
        low = [jnp.where(narrow, t[j], r[j + 1]) for j in (0, 2)]
        high = [jnp.where(narrow, r[j], t[j + 1]) for j in (0, 2)]
        fsend[2 * b] = jnp.concatenate(low, axis=0).astype(BF16)
        fsend[2 * b + 1] = jnp.concatenate(high, axis=0).astype(BF16)
    f_copies = []
    for i in range(LO):
        copy = remote(
            fsend.at[i], frecv.at[z // LO], f_send.at[i], f_rcv.at[z // LO], finals[i]
        )
        f_copies.append(copy)

        @pl.when(jnp.logical_not(final_self[i]))
        def _(copy=copy):
            copy.start()

        @pl.when(final_self[i])
        def _(i=i):
            copy = pltpu.make_async_copy(fsend.at[i], frecv.at[z // LO], f_rcv.at[z // LO])
            copy.start()
            copy.wait()

    arrived_core(4)
    multiply(4, oc)
    arrived_core(5)
    multiply(5, oc)
    val_ref[...] = vacc[...].astype(BF16)
    out_copies = [
        pltpu.make_async_copy(tg_ref, tg_hbm, out_sem.at[0]),
        pltpu.make_async_copy(val_ref, val_hbm, out_sem.at[1]),
    ]
    for copy in out_copies:
        copy.start()

    for g in range(4):
        @pl.when(jnp.logical_not(source_self[g]))
        def _(g=g):
            remote(fsend.at[0], frecv.at[g], f_send.at[g], f_rcv.at[g], to_core).wait_recv()

    for copy in (
        core_copies + tx_copies + tz_copies + ux_copies + uz_copies + [up_own] + uc_copies
        + w_copies + zout_copies + xout_copies + y_copies
    ):
        copy.wait_send()
    for i in range(LO):
        @pl.when(jnp.logical_not(final_self[i]))
        def _(i=i):
            f_copies[i].wait_send()
    for copy in out_copies:
        copy.wait()


def writer(val_in, tg_in, last_in, val_out, tg_out, wg_out, val, tg, last, wg, in_sem, out_sem):
    pieces = [(last_in, last, wg_out), (val_in, val, val_out)]
    for i in range(4):
        rows = pl.ds(i * (TOK // 4), TOK // 4)
        pieces.append((tg_in.at[rows], tg.at[rows], tg_out.at[rows]))
    ins = [pltpu.make_async_copy(a, b, in_sem.at[i]) for i, (a, b, _) in enumerate(pieces)]
    outs = [
        pltpu.make_async_copy(wg if i == 0 else b, c, out_sem.at[i])
        for i, (_, b, c) in enumerate(pieces)
    ]
    for copy in ins:
        copy.start()
    ins[0].wait()
    final = (last[0].astype(F32) + last[1].astype(F32)) + (
        last[2].astype(F32) + last[3].astype(F32)
    )
    for j in range(2):
        block = final[8 * j : 8 * j + 8, :]
        wg[:, 256 * j : 256 * j + 128] = block[0:4, :]
        wg[:, 256 * j + 128 : 256 * j + 256] = pltpu.roll(block, 4, 0)[0:4, :]
    outs[0].start()
    for i in range(1, len(ins)):
        ins[i].wait()
        outs[i].start()
    for copy in outs:
        copy.wait()


def write_out(results):
    any_space = pl.BlockSpec(memory_space=pltpu.HBM)
    shapes = (((TOK, KV), BF16), ((TOK, D), BF16), ((4, KV), F32))
    return pl.pallas_call(
        writer,
        out_shape=tuple(jax.ShapeDtypeStruct(*shape) for shape in shapes),
        in_specs=[any_space] * 3,
        out_specs=(any_space,) * 3,
        scratch_shapes=[
            pltpu.VMEM((TOK, KV), BF16),
            pltpu.VMEM((TOK, D), BF16),
            pltpu.VMEM((4, 16, 128), BF16),
            pltpu.VMEM((4, KV), F32),
        ]
        + [pltpu.SemaphoreType.DMA((6,))] * 2,
        compiler_params=pltpu.CompilerParams(vmem_limit_bytes=60 * 1024 * 1024),
    )(*results)


def body(tokens, weight_codes, weight_scales, grad_codes, grad_scales):
    any_space = pl.BlockSpec(memory_space=pltpu.HBM)
    vmem = pl.BlockSpec(memory_space=pltpu.VMEM)
    dma = pltpu.SemaphoreType.DMA
    results = pl.pallas_call(
        kernel,
        out_shape=(
            jax.ShapeDtypeStruct((TOK, KV), BF16),
            jax.ShapeDtypeStruct((TOK, D), BF16),
            jax.ShapeDtypeStruct((4, 16, 128), BF16),
        ),
        in_specs=[any_space, any_space, vmem, any_space, vmem],
        out_specs=(any_space, any_space, any_space),
        scratch_shapes=[
            pltpu.VMEM((TOK, KV), BF16),
            pltpu.VMEM((TOK, D), BF16),
            pltpu.VMEM((TOK, D), BF16),
            pltpu.VMEM((ROWS, KV), jnp.int32),
            pltpu.VMEM((TOK, KV), jnp.int32),
            pltpu.VMEM((8, ROWS, KV), BF16),
            pltpu.VMEM((1024, 256), BF16),
            pltpu.VMEM((1024, 256), BF16),
            pltpu.VMEM((1024, KV), BF16),
            pltpu.VMEM((1024, KV), BF16),
            pltpu.VMEM((TOK, KV), F32),
            pltpu.VMEM((256, KV), F32),
            pltpu.VMEM((256, KV), F32),
            pltpu.VMEM((3, 64, KV), BF16),
            pltpu.VMEM((3, 64, KV), BF16),
            pltpu.VMEM((64, KV), F32),
            pltpu.VMEM((3, 64, KV), BF16),
            pltpu.VMEM((3, 64, KV), BF16),
            pltpu.VMEM((64, KV), F32),
            pltpu.VMEM((NY, 16, KV), BF16),
            pltpu.VMEM((NY - 1, 16, KV), BF16),
            pltpu.VMEM((4, 16, 128), BF16),
        ]
        + [
            dma((n,))
            for n in (3, 4, 4, 4, 12, 12, 16, 16, 4, 4, 4, 4, 8, 8, 6, 6, 8, 8, 4, 4, 3, 3, 7, 7, 4, 4, 2)
        ],
        compiler_params=pltpu.CompilerParams(
            collective_id=0, has_side_effects=True, vmem_limit_bytes=60 * 1024 * 1024
        ),
    )(tokens, weight_codes, weight_scales, grad_codes, grad_scales.T)
    return write_out(results)


def solution(mesh):
    return jax.shard_map(
        body,
        mesh=mesh,
        in_specs=(
            P(("hst", "outer"), None),
            P("hst", None),
            P("hst", None),
            P(("hst", "outer"), None),
            P(("hst", "outer"), None),
        ),
        out_specs=(P(("hst", "outer"), None), P(("hst", "outer"), None), P(("hst", "outer"), None)),
        check_vma=False,
    )
```

```python
import jax
import jax.numpy as jnp
from jax import lax
from jax.experimental import pallas as pl
from jax.experimental.pallas import tpu as pltpu
from jax.sharding import PartitionSpec as P

F32, BF16 = jnp.float32, jnp.bfloat16
NX, NY, NZ = 4, 8, 16
LO = 4
TOK, D, KV, ROWS, HEADS = 128, 4096, 512, 512, 4
HALF = ROWS // 2
XSTEPS, XFIRST, XCOUNT = (1, 3, 2), (256, 512, 768), (128, 128, 128)
ZSTEPS, ZFIRST, ZCOUNT = (1, -1, 2, -2), (256, 512, 768, 896), (128, 128, 64, 64)


def kernel(
    tok_hbm, wc_hbm, ws_ref, gc_hbm, gs_ref,
    val_hbm, tg_hbm, frecv,
    val_ref, tg_ref, tok, wc, gc, wbuf, tx, tz, ux, uz, vacc, term_x, term_z,
    zout, zin, zown, xout, xin, xown, ysend, yrecv, fsend,
    in_sem, own_sem, core_tsend, core_trcv, tx_send, tx_rcv, tz_send, tz_rcv,
    ux_send, ux_rcv, uz_send, uz_rcv, uc_send, uc_rcv,
    wsend, wrcv, wcsend, wcrcv, z_send, z_rcv, x_send, x_rcv, y_send, y_rcv, f_send, f_rcv, out_sem, far1, far2, far3,
):
    h, o = lax.axis_index("hst"), lax.axis_index("outer")
    c, ylo = lax.rem(h, 2), h // 2
    yhi, x, z = lax.rem(o, 2), lax.rem(o // 2, NX), o // (2 * NX)
    y = yhi * LO + ylo
    oc = 1 - c
    klass = lax.rem(z, LO)

    def dev(x, y, z, c):
        return (lax.rem(y, LO) * 2 + c, (z * NX + x) * 2 + y // LO)

    def at_z(step):
        return lax.rem(z + step + NZ, NZ)

    def at_y(step):
        return lax.rem(y + step + NY, NY)

    def at_x(step):
        return lax.rem(x + step, NX)

    def remote(src, dst, ssem, rsem, to):
        return pltpu.make_async_remote_copy(
            src_ref=src, dst_ref=dst, send_sem=ssem, recv_sem=rsem,
            device_id=to, device_id_type=pl.DeviceIdType.MESH,
        )

    def signal(sem, to):
        pl.semaphore_signal(sem, inc=1, device_id=to, device_id_type=pl.DeviceIdType.MESH)

    by_x = ylo < 2
    final_x = jnp.where(by_x, klass, x)
    final_q = jnp.where(by_x, x, klass)
    finals = [dev(final_x, y, final_q * LO + i, c) for i in range(LO)]
    final_self = [(final_x == x) & (final_q * LO + i == z) for i in range(LO)]
    source_x = jnp.where(by_x, z // LO, x)
    source_k = jnp.where(by_x, x, z // LO)
    sources = [dev(source_x, y, source_k + LO * g, c) for g in range(4)]
    source_self = [(source_x == x) & (source_k + LO * g == z) for g in range(4)]

    to_left, to_right = dev(x, at_y(-1), z, c), dev(x, at_y(1), z, c)

    load_tok = pltpu.make_async_copy(tok_hbm, tok, in_sem.at[0])
    load_wc = pltpu.make_async_copy(wc_hbm, wc, in_sem.at[1])
    load_gc = pltpu.make_async_copy(gc_hbm, gc, in_sem.at[2])
    load_gc.start()
    load_wc.start()
    load_tok.start()

    def columns(ylo_of, cc, q):
        return pl.ds(pl.multiple_of(((ylo_of * 2 + cc) * 4 + q) * 128, 128), 128)

    own_copies = []
    for j in range(2):
        lanes = pl.ds(j * 128, 128)
        own_copies.append(pltpu.make_async_copy(
            tok_hbm.at[:, columns(j, c, x)], tx.at[pl.ds(0, TOK), lanes], own_sem.at[j]
        ))
        own_copies.append(pltpu.make_async_copy(
            tok_hbm.at[:, columns(2 + j, c, klass)], tz.at[pl.ds(0, TOK), lanes], own_sem.at[2 + j]
        ))
    for copy in own_copies:
        copy.start()

    barrier = pltpu.get_barrier_semaphore()
    partners = [dev(at_x(s), y, z, cc) for s in (2, 1, 3) for cc in (c, oc)]
    partners += [dev(x, y, at_z(s), cc) for s in (2, -2, 1, -1) for cc in (c, oc)]
    partners += [dev(x, at_y(1), z, c), dev(x, at_y(-1), z, c), dev(x, y, z, oc)]
    for p in partners:
        signal(barrier, p)
    load_gc.wait()
    scales = gs_ref[...].T
    for k in range(HEADS):
        lanes = slice(k * 128, (k + 1) * 128)
        ux[0:TOK, lanes] = (gc[:, lanes].astype(F32) * scales[:, k : k + 1]).astype(BF16)
    pl.semaphore_wait(barrier, len(partners))
    for to in (dev(x, y, at_z(2), c), dev(x, y, at_z(-2), c), to_left, to_right):
        signal(far1, to)

    core_copies, tx_copies, tz_copies = [], [], []
    for j in range(2):
        lanes = pl.ds(j * 128, 128)
        core_copies.append(remote(
            tok_hbm.at[:, columns(j, oc, x)], tx.at[pl.ds(TOK, TOK), lanes],
            core_tsend.at[j], core_trcv.at[j], dev(x, y, z, oc),
        ))
        core_copies.append(remote(
            tok_hbm.at[:, columns(2 + j, oc, klass)], tz.at[pl.ds(TOK, TOK), lanes],
            core_tsend.at[2 + j], core_trcv.at[2 + j], dev(x, y, z, oc),
        ))
    for i, s in enumerate(XSTEPS):
        for k, cc in enumerate((c, oc)):
            for j in range(2):
                tx_copies.append(remote(
                    tok_hbm.at[:, columns(j, cc, at_x(s))],
                    tx.at[pl.ds(XFIRST[i] + k * XCOUNT[i], XCOUNT[i]), pl.ds(j * 128, 128)],
                    tx_send.at[4 * i + 2 * k + j], tx_rcv.at[4 * i + 2 * k + j],
                    dev(at_x(s), y, z, cc),
                ))
    for i, s in enumerate(ZSTEPS):
        first = 64 if s == -2 else 0
        for k, cc in enumerate((c, oc)):
            for j in range(2):
                tz_copies.append(remote(
                    tok_hbm.at[pl.ds(first, ZCOUNT[i]), columns(2 + j, cc, lax.rem(at_z(s), LO))],
                    tz.at[pl.ds(ZFIRST[i] + k * ZCOUNT[i], ZCOUNT[i]), pl.ds(j * 128, 128)],
                    tz_send.at[4 * i + 2 * k + j], tz_rcv.at[4 * i + 2 * k + j],
                    dev(x, y, at_z(s), cc),
                ))

    to_core = dev(x, y, z, oc)
    up_own = remote(
        ux.at[pl.ds(0, TOK)], ux.at[pl.ds(TOK, TOK)], uc_send.at[7], uc_rcv.at[7], to_core
    )
    ux_copies, uz_copies = [], []
    for i, s in enumerate((1, 3)):
        ux_copies.append(remote(
            ux.at[pl.ds(0, TOK)], ux.at[pl.ds(XFIRST[i], TOK)],
            ux_send.at[i], ux_rcv.at[i], dev(at_x(s), y, z, c),
        ))
    for i, s in enumerate((1, -1)):
        uz_copies.append(remote(
            ux.at[pl.ds(0, TOK)], uz.at[pl.ds(ZFIRST[i], TOK)],
            uz_send.at[i], uz_rcv.at[i], dev(x, y, at_z(s), c),
        ))
    for i, s in enumerate((1, 3)):
        ux_copies.append(remote(
            ux.at[pl.ds(XFIRST[i] + 64 * i, 64)], ux.at[pl.ds(XFIRST[2] + 64 * i, 64)],
            ux_send.at[2 + i], ux_rcv.at[2 + i], dev(at_x(s), y, z, c),
        ))
    for i, s in enumerate((1, -1)):
        uz_copies.append(remote(
            uz.at[pl.ds(ZFIRST[i] + 64 * i, 64)], uz.at[pl.ds(ZFIRST[2 + i], 64)],
            uz_send.at[2 + i], uz_rcv.at[2 + i], dev(x, y, at_z(s), c),
        ))
    for copy in ux_copies[:2] + uz_copies[:2] + [up_own]:
        copy.start()
    for copy in tx_copies[8:] + tz_copies[8:] + core_copies + tx_copies[:8] + tz_copies[:8]:
        copy.start()
    uc_copies = [
        remote(
            ux.at[pl.ds(XFIRST[i], TOK)], ux.at[pl.ds(XFIRST[i] + TOK, TOK)],
            uc_send.at[i], uc_rcv.at[i], to_core,
        )
        for i in range(3)
    ] + [
        remote(
            uz.at[pl.ds(ZFIRST[i], ZCOUNT[i])], uz.at[pl.ds(ZFIRST[i] + ZCOUNT[i], ZCOUNT[i])],
            uc_send.at[3 + i], uc_rcv.at[3 + i], to_core,
        )
        for i in range(4)
    ]


    load_wc.wait()
    for b in range(ROWS // 128):
        rows = slice(b * 128, (b + 1) * 128)
        wbuf[h, rows, :] = (wc[rows, :].astype(F32) * ws_ref[b : b + 1, :]).astype(BF16)

    def part(ylo_of, cc, half):
        return wbuf.at[ylo_of * 2 + cc, pl.ds(half * HALF, HALF)]

    left, right, far = lax.rem(ylo + 3, LO), lax.rem(ylo + 1, LO), lax.rem(ylo + 2, LO)
    w_copies = []

    def send_w(which, half, ssem, rsem, to):
        src = part(which, c, half)
        copy = remote(src, src, ssem, rsem, to)
        copy.start()
        w_copies.append(copy)

    send_w(ylo, 0, wsend.at[0], wrcv.at[0], to_right)
    send_w(ylo, 1, wsend.at[3], wrcv.at[3], to_left)
    send_w(ylo, 1, wsend.at[1], wrcv.at[1], to_right)
    send_w(ylo, 0, wsend.at[2], wrcv.at[2], to_left)
    send_w(ylo, 0, wcsend.at[6], wcrcv.at[6], to_core)
    send_w(ylo, 1, wcsend.at[7], wcrcv.at[7], to_core)
    where = ((left, 0), (left, 1), (right, 0), (right, 1), (far, 0), (far, 1), (ylo, 0), (ylo, 1))

    def arrived(i):
        which, half = where[i]
        ref = part(which, c, half)
        remote(ref, ref, wsend.at[i], wrcv.at[i], to_core).wait_recv()

    def arrived_core(i):
        which, half = where[i]
        ref = part(which, oc, half)
        remote(ref, ref, wcsend.at[i], wcrcv.at[i], to_core).wait_recv()

    def pass_on(i):
        which, half = where[i]
        send_w(which, half, wcsend.at[i], wcrcv.at[i], to_core)

    load_tok.wait()
    vacc[...] = jnp.zeros_like(vacc)

    def multiply(i, cc):
        which, half = where[i]
        slot = which * 2 + cc
        lanes = pl.ds(pl.multiple_of(slot * ROWS + half * HALF, HALF), HALF)
        piece = wbuf[slot, half * HALF : (half + 1) * HALF, :]
        vacc[...] += jnp.dot(tok[:, lanes], piece, preferred_element_type=F32)
        tg_ref[:, lanes] = lax.dot_general(
            ux[0:TOK, :], piece, (((1,), (1,)), ((), ())), preferred_element_type=F32
        ).astype(BF16)

    def product(tokens, upstream, first):
        return lax.dot_general(
            tokens[first : first + 256, :], upstream[first : first + 256, :],
            (((0,), (0,)), ((), ())), preferred_element_type=F32,
        )

    def up_pass_on(copy, i):
        copy.wait_recv()
        uc_copies[i].start()

    for i in (0, 1):
        ux_copies[i].wait_recv()
        ux_copies[2 + i].start()
        uc_copies[i].start()
        uz_copies[i].wait_recv()
        uz_copies[2 + i].start()
        uc_copies[3 + i].start()

    pl.semaphore_wait(far1, 4)
    for to in (
        dev(x, y, at_z(4), c), dev(x, y, at_z(-4), c), dev(x, at_y(2), z, c), dev(x, at_y(-2), z, c)
    ):
        signal(far2, to)
    arrived(0)
    send_w(left, 0, wsend.at[4], wrcv.at[4], to_right)
    pass_on(0)
    arrived(3)
    send_w(right, 1, wsend.at[5], wrcv.at[5], to_left)
    pass_on(3)
    multiply(6, c)
    multiply(7, c)
    for copy in own_copies:
        copy.wait()
    for copy in core_copies + [up_own]:
        copy.wait_recv()
    term_x[...] = product(tx, ux, 0)
    term_z[...] = product(tz, ux, 0)
    ux_copies[2].wait_recv()
    up_pass_on(ux_copies[3], 2)
    up_pass_on(uz_copies[2], 5)
    up_pass_on(uz_copies[3], 6)
    arrived_core(6)
    multiply(6, oc)
    arrived_core(7)
    multiply(7, oc)
    multiply(0, c)
    multiply(3, c)

    def wait_x(i):
        for copy in tx_copies[4 * i : 4 * i + 4] + [uc_copies[i]]:
            copy.wait_recv()

    def wait_z(i):
        for copy in tz_copies[4 * i : 4 * i + 4] + [uc_copies[3 + i]]:
            copy.wait_recv()

    for i in range(2):
        wait_x(i)
        term_x[...] += product(tx, ux, XFIRST[i])
        wait_z(i)
        term_z[...] += product(tz, uz, ZFIRST[i])

    def of_x(term, xx):
        rows = [term[pl.ds(pl.multiple_of(a * 32 + xx * 8, 8), 8), :] for a in range(8)]
        return jnp.concatenate(rows, axis=0)

    wait_x(2)
    term_x[...] += product(tx, ux, XFIRST[2])
    zout_copies = []
    for i, s in enumerate((2, 1, -1)):
        zout[i] = of_x(term_x, lax.rem(at_z(s), LO)).astype(BF16)
        if s == 2:
            pieces = ((0, 32, 2, 2, 2), (32, 32, -2, 2, 3))
        else:
            pieces = ((0, 64, s, 0 if s == 1 else 1, 0 if s == 1 else 1),)
        for first, count, step, slot, sem in pieces:
            copy = remote(
                zout.at[i, pl.ds(first, count)], zin.at[slot, pl.ds(first, count)],
                z_send.at[sem], z_rcv.at[sem], dev(x, y, at_z(step), c),
            )
            copy.start()
            zout_copies.append(copy)
    zown[...] = of_x(term_x, klass)
    wait_z(2)
    wait_z(3)
    term_z[...] += product(tz, uz, ZFIRST[2])
    xout_copies = []
    for i, s in enumerate((2, 1, 3)):
        xout[i] = of_x(term_z, at_x(s)).astype(BF16)
        copy = remote(
            xout.at[i], xin.at[i], x_send.at[i], x_rcv.at[i], dev(at_x(s), y, z, c)
        )
        copy.start()
        xout_copies.append(copy)
    xown[...] = of_x(term_z, x)

    pl.semaphore_wait(far2, 4)
    for s in range(1, NX):
        signal(far3, dev(at_x(s), y, z, c))
    arrived(1)
    pass_on(1)
    arrived(2)
    pass_on(2)
    multiply(1, c)
    multiply(2, c)
    arrived_core(0)
    multiply(0, oc)
    arrived_core(3)
    multiply(3, oc)

    upper = lax.broadcasted_iota(jnp.int32, (8, KV), 0) < 4

    def regroup(total, first_ylo):
        for j in range(2):
            low, high = [], []
            for k in range(2):
                row = j * 32 + k * 16
                a, b = total[row : row + 8, :], total[row + 8 : row + 16, :]
                low.append(jnp.where(upper, a, pltpu.roll(b, 4, 0)))
                high.append(jnp.where(upper, pltpu.roll(a, 4, 0), b))
            ysend[first_ylo + j] = jnp.concatenate(low, axis=0).astype(BF16)
            ysend[LO + first_ylo + j] = jnp.concatenate(high, axis=0).astype(BF16)

    for copy in zout_copies:
        copy.wait_recv()
    regroup(
        (zown[...] + zin[0].astype(F32)) + (zin[1].astype(F32) + zin[2].astype(F32)), 0
    )
    for copy in xout_copies:
        copy.wait_recv()
    regroup(
        (xown[...] + xin[0].astype(F32)) + (xin[1].astype(F32) + xin[2].astype(F32)), 2
    )
    y_copies = []
    for s in (4, 3, 5, 2, 6, 1, 7):
        copy = remote(
            ysend.at[at_y(s)], yrecv.at[s - 1], y_send.at[s - 1], y_rcv.at[s - 1],
            dev(x, at_y(s), z, c),
        )
        copy.start()
        y_copies.append(copy)

    arrived(4)
    pass_on(4)
    arrived(5)
    pass_on(5)
    multiply(4, c)
    multiply(5, c)
    arrived_core(1)
    multiply(1, oc)
    arrived_core(2)
    multiply(2, oc)

    for copy in y_copies:
        copy.wait_recv()
    total = ysend[y].astype(F32)
    for s in range(NY - 1):
        total += yrecv[s].astype(F32)
    narrow = lax.broadcasted_iota(jnp.int32, (8, 128), 0) < 4
    for b in range(2):
        t = [total[8 * b : 8 * b + 8, 128 * j : 128 * j + 128] for j in range(4)]
        r = [pltpu.roll(a, 4, 0) for a in t]
        low = [jnp.where(narrow, t[j], r[j + 1]) for j in (0, 2)]
        high = [jnp.where(narrow, r[j], t[j + 1]) for j in (0, 2)]
        fsend[2 * b] = jnp.concatenate(low, axis=0).astype(BF16)
        fsend[2 * b + 1] = jnp.concatenate(high, axis=0).astype(BF16)
    pl.semaphore_wait(far3, NX - 1)
    f_copies = []
    for i in range(LO):
        copy = remote(
            fsend.at[i], frecv.at[z // LO], f_send.at[i], f_rcv.at[z // LO], finals[i]
        )
        f_copies.append(copy)

        @pl.when(jnp.logical_not(final_self[i]))
        def _(copy=copy):
            copy.start()

        @pl.when(final_self[i])
        def _(i=i):
            copy = pltpu.make_async_copy(fsend.at[i], frecv.at[z // LO], f_rcv.at[z // LO])
            copy.start()
            copy.wait()

    arrived_core(4)
    multiply(4, oc)
    arrived_core(5)
    multiply(5, oc)
    val_ref[...] = vacc[...].astype(BF16)
    out_copies = [
        pltpu.make_async_copy(tg_ref, tg_hbm, out_sem.at[0]),
        pltpu.make_async_copy(val_ref, val_hbm, out_sem.at[1]),
    ]
    for copy in out_copies:
        copy.start()

    for g in range(4):
        @pl.when(jnp.logical_not(source_self[g]))
        def _(g=g):
            remote(fsend.at[0], frecv.at[g], f_send.at[g], f_rcv.at[g], to_core).wait_recv()

    for copy in (
        core_copies + tx_copies + tz_copies + ux_copies + uz_copies + [up_own] + uc_copies
        + w_copies + zout_copies + xout_copies + y_copies
    ):
        copy.wait_send()
    for i in range(LO):
        @pl.when(jnp.logical_not(final_self[i]))
        def _(i=i):
            f_copies[i].wait_send()
    for copy in out_copies:
        copy.wait()


def writer(val_in, tg_in, last_in, val_out, tg_out, wg_out, val, tg, last, wg, in_sem, out_sem):
    pieces = [(last_in, last, wg_out), (val_in, val, val_out)]
    for i in range(4):
        rows = pl.ds(i * (TOK // 4), TOK // 4)
        pieces.append((tg_in.at[rows], tg.at[rows], tg_out.at[rows]))
    ins = [pltpu.make_async_copy(a, b, in_sem.at[i]) for i, (a, b, _) in enumerate(pieces)]
    outs = [
        pltpu.make_async_copy(wg if i == 0 else b, c, out_sem.at[i])
        for i, (_, b, c) in enumerate(pieces)
    ]
    for copy in ins:
        copy.start()
    ins[0].wait()
    final = (last[0].astype(F32) + last[1].astype(F32)) + (
        last[2].astype(F32) + last[3].astype(F32)
    )
    for j in range(2):
        block = final[8 * j : 8 * j + 8, :]
        wg[:, 256 * j : 256 * j + 128] = block[0:4, :]
        wg[:, 256 * j + 128 : 256 * j + 256] = pltpu.roll(block, 4, 0)[0:4, :]
    outs[0].start()
    for i in range(1, len(ins)):
        ins[i].wait()
        outs[i].start()
    for copy in outs:
        copy.wait()


def write_out(results):
    any_space = pl.BlockSpec(memory_space=pltpu.HBM)
    shapes = (((TOK, KV), BF16), ((TOK, D), BF16), ((4, KV), F32))
    return pl.pallas_call(
        writer,
        out_shape=tuple(jax.ShapeDtypeStruct(*shape) for shape in shapes),
        in_specs=[any_space] * 3,
        out_specs=(any_space,) * 3,
        scratch_shapes=[
            pltpu.VMEM((TOK, KV), BF16),
            pltpu.VMEM((TOK, D), BF16),
            pltpu.VMEM((4, 16, 128), BF16),
            pltpu.VMEM((4, KV), F32),
        ]
        + [pltpu.SemaphoreType.DMA((6,))] * 2,
        compiler_params=pltpu.CompilerParams(vmem_limit_bytes=60 * 1024 * 1024),
    )(*results)


def body(tokens, weight_codes, weight_scales, grad_codes, grad_scales):
    any_space = pl.BlockSpec(memory_space=pltpu.HBM)
    vmem = pl.BlockSpec(memory_space=pltpu.VMEM)
    dma = pltpu.SemaphoreType.DMA
    results = pl.pallas_call(
        kernel,
        out_shape=(
            jax.ShapeDtypeStruct((TOK, KV), BF16),
            jax.ShapeDtypeStruct((TOK, D), BF16),
            jax.ShapeDtypeStruct((4, 16, 128), BF16),
        ),
        in_specs=[any_space, any_space, vmem, any_space, vmem],
        out_specs=(any_space, any_space, any_space),
        scratch_shapes=[
            pltpu.VMEM((TOK, KV), BF16),
            pltpu.VMEM((TOK, D), BF16),
            pltpu.VMEM((TOK, D), BF16),
            pltpu.VMEM((ROWS, KV), jnp.int32),
            pltpu.VMEM((TOK, KV), jnp.int32),
            pltpu.VMEM((8, ROWS, KV), BF16),
            pltpu.VMEM((1024, 256), BF16),
            pltpu.VMEM((1024, 256), BF16),
            pltpu.VMEM((1024, KV), BF16),
            pltpu.VMEM((1024, KV), BF16),
            pltpu.VMEM((TOK, KV), F32),
            pltpu.VMEM((256, KV), F32),
            pltpu.VMEM((256, KV), F32),
            pltpu.VMEM((3, 64, KV), BF16),
            pltpu.VMEM((3, 64, KV), BF16),
            pltpu.VMEM((64, KV), F32),
            pltpu.VMEM((3, 64, KV), BF16),
            pltpu.VMEM((3, 64, KV), BF16),
            pltpu.VMEM((64, KV), F32),
            pltpu.VMEM((NY, 16, KV), BF16),
            pltpu.VMEM((NY - 1, 16, KV), BF16),
            pltpu.VMEM((4, 16, 128), BF16),
        ]
        + [
            dma((n,))
            for n in (3, 4, 4, 4, 12, 12, 16, 16, 4, 4, 4, 4, 8, 8, 6, 6, 8, 8, 4, 4, 3, 3, 7, 7, 4, 4, 2)
        ]
        + [pltpu.SemaphoreType.REGULAR] * 3,
        compiler_params=pltpu.CompilerParams(
            collective_id=0, has_side_effects=True, vmem_limit_bytes=60 * 1024 * 1024
        ),
    )(tokens, weight_codes, weight_scales, grad_codes, grad_scales.T)
    return write_out(results)


def solution(mesh):
    return jax.shard_map(
        body,
        mesh=mesh,
        in_specs=(
            P(("hst", "outer"), None),
            P("hst", None),
            P("hst", None),
            P(("hst", "outer"), None),
            P(("hst", "outer"), None),
        ),
        out_specs=(P(("hst", "outer"), None), P(("hst", "outer"), None), P(("hst", "outer"), None)),
        check_vma=False,
    )
```

```python
import jax
import jax.numpy as jnp
from jax import lax
from jax.experimental import pallas as pl
from jax.experimental.pallas import tpu as pltpu
from jax.sharding import PartitionSpec as P

F32, BF16 = jnp.float32, jnp.bfloat16
NX, NY, NZ = 4, 8, 16
LO = 4
TOK, D, KV, ROWS, HEADS = 128, 4096, 512, 512, 4
HALF = ROWS // 2
XSTEPS, XFIRST, XCOUNT = (1, 3, 2), (256, 512, 768), (128, 128, 128)
ZSTEPS, ZFIRST, ZCOUNT = (1, -1, 2, -2), (256, 512, 768, 896), (128, 128, 64, 64)


def kernel(
    tok_hbm, wc_hbm, ws_hbm, gc_hbm, gs_hbm,
    val_hbm, tg_hbm, frecv,
    val_ref, tg_ref, tok, wc, gc, wbuf, tx, tz, ux, uz, vacc, term_x, term_z,
    zout, zin, zown, xout, xin, xown, ysend, yrecv, fsend, ws_ref, gs_ref,
    in_sem, own_sem, core_tsend, core_trcv, tx_send, tx_rcv, tz_send, tz_rcv,
    ux_send, ux_rcv, uz_send, uz_rcv, uc_send, uc_rcv,
    wsend, wrcv, wcsend, wcrcv, z_send, z_rcv, x_send, x_rcv, y_send, y_rcv, f_send, f_rcv, out_sem, far1, far2, far3, far4,
):
    h, o = lax.axis_index("hst"), lax.axis_index("outer")
    c, ylo = lax.rem(h, 2), h // 2
    yhi, x, z = lax.rem(o, 2), lax.rem(o // 2, NX), o // (2 * NX)
    y = yhi * LO + ylo
    oc = 1 - c
    klass = lax.rem(z, LO)

    def dev(x, y, z, c):
        return (lax.rem(y, LO) * 2 + c, (z * NX + x) * 2 + y // LO)

    def at_z(step):
        return lax.rem(z + step + NZ, NZ)

    def at_y(step):
        return lax.rem(y + step + NY, NY)

    def at_x(step):
        return lax.rem(x + step, NX)

    def remote(src, dst, ssem, rsem, to):
        return pltpu.make_async_remote_copy(
            src_ref=src, dst_ref=dst, send_sem=ssem, recv_sem=rsem,
            device_id=to, device_id_type=pl.DeviceIdType.MESH,
        )

    def signal(sem, to):
        pl.semaphore_signal(sem, inc=1, device_id=to, device_id_type=pl.DeviceIdType.MESH)

    by_x = ylo < 2
    final_x = jnp.where(by_x, klass, x)
    final_q = jnp.where(by_x, x, klass)
    finals = [dev(final_x, y, final_q * LO + i, c) for i in range(LO)]
    final_self = [(final_x == x) & (final_q * LO + i == z) for i in range(LO)]
    source_x = jnp.where(by_x, z // LO, x)
    source_k = jnp.where(by_x, x, z // LO)
    sources = [dev(source_x, y, source_k + LO * g, c) for g in range(4)]
    source_self = [(source_x == x) & (source_k + LO * g == z) for g in range(4)]

    to_left, to_right = dev(x, at_y(-1), z, c), dev(x, at_y(1), z, c)

    barrier = pltpu.get_barrier_semaphore()
    partners = [dev(at_x(s), y, z, cc) for s in (1, 3) for cc in (c, oc)]
    partners += [dev(x, y, at_z(s), cc) for s in (1, -1) for cc in (c, oc)]
    partners += [dev(x, at_y(1), z, c), dev(x, at_y(-1), z, c), dev(x, y, z, oc)]
    for p in partners:
        signal(barrier, p)

    load_tok = pltpu.make_async_copy(tok_hbm, tok, in_sem.at[0])
    load_wc = pltpu.make_async_copy(wc_hbm, wc, in_sem.at[1])
    load_gc = pltpu.make_async_copy(gc_hbm, gc, in_sem.at[2])
    load_gs = pltpu.make_async_copy(gs_hbm, gs_ref, in_sem.at[3])
    load_ws = pltpu.make_async_copy(ws_hbm, ws_ref, in_sem.at[4])
    for copy in (load_gc, load_gs, load_wc, load_ws, load_tok):
        copy.start()

    def columns(ylo_of, cc, q):
        return pl.ds(pl.multiple_of(((ylo_of * 2 + cc) * 4 + q) * 128, 128), 128)

    own_copies = []
    for j in range(2):
        lanes = pl.ds(j * 128, 128)
        own_copies.append(pltpu.make_async_copy(
            tok_hbm.at[:, columns(j, c, x)], tx.at[pl.ds(0, TOK), lanes], own_sem.at[j]
        ))
        own_copies.append(pltpu.make_async_copy(
            tok_hbm.at[:, columns(2 + j, c, klass)], tz.at[pl.ds(0, TOK), lanes], own_sem.at[2 + j]
        ))
    for copy in own_copies:
        copy.start()

    load_gc.wait()
    load_gs.wait()
    scales = gs_ref[...].T
    for k in range(HEADS):
        lanes = slice(k * 128, (k + 1) * 128)
        ux[0:TOK, lanes] = (gc[:, lanes].astype(F32) * scales[:, k : k + 1]).astype(BF16)
    pl.semaphore_wait(barrier, len(partners))
    for to in (
        dev(x, y, at_z(1), c), dev(x, y, at_z(-1), c), dev(at_x(1), y, z, c), dev(at_x(3), y, z, c),
        to_left, to_right,
    ):
        signal(far1, to)

    core_copies, tx_copies, tz_copies = [], [], []
    for j in range(2):
        lanes = pl.ds(j * 128, 128)
        core_copies.append(remote(
            tok_hbm.at[:, columns(j, oc, x)], tx.at[pl.ds(TOK, TOK), lanes],
            core_tsend.at[j], core_trcv.at[j], dev(x, y, z, oc),
        ))
        core_copies.append(remote(
            tok_hbm.at[:, columns(2 + j, oc, klass)], tz.at[pl.ds(TOK, TOK), lanes],
            core_tsend.at[2 + j], core_trcv.at[2 + j], dev(x, y, z, oc),
        ))
    for i, s in enumerate(XSTEPS):
        for k, cc in enumerate((c, oc)):
            for j in range(2):
                tx_copies.append(remote(
                    tok_hbm.at[:, columns(j, cc, at_x(s))],
                    tx.at[pl.ds(XFIRST[i] + k * XCOUNT[i], XCOUNT[i]), pl.ds(j * 128, 128)],
                    tx_send.at[4 * i + 2 * k + j], tx_rcv.at[4 * i + 2 * k + j],
                    dev(at_x(s), y, z, cc),
                ))
    for i, s in enumerate(ZSTEPS):
        first = 64 if s == -2 else 0
        for k, cc in enumerate((c, oc)):
            for j in range(2):
                tz_copies.append(remote(
                    tok_hbm.at[pl.ds(first, ZCOUNT[i]), columns(2 + j, cc, lax.rem(at_z(s), LO))],
                    tz.at[pl.ds(ZFIRST[i] + k * ZCOUNT[i], ZCOUNT[i]), pl.ds(j * 128, 128)],
                    tz_send.at[4 * i + 2 * k + j], tz_rcv.at[4 * i + 2 * k + j],
                    dev(x, y, at_z(s), cc),
                ))

    to_core = dev(x, y, z, oc)
    up_own = remote(
        ux.at[pl.ds(0, TOK)], ux.at[pl.ds(TOK, TOK)], uc_send.at[7], uc_rcv.at[7], to_core
    )
    ux_copies, uz_copies = [], []
    for i, s in enumerate((1, 3)):
        ux_copies.append(remote(
            ux.at[pl.ds(0, TOK)], ux.at[pl.ds(XFIRST[i], TOK)],
            ux_send.at[i], ux_rcv.at[i], dev(at_x(s), y, z, c),
        ))
    for i, s in enumerate((1, -1)):
        uz_copies.append(remote(
            ux.at[pl.ds(0, TOK)], uz.at[pl.ds(ZFIRST[i], TOK)],
            uz_send.at[i], uz_rcv.at[i], dev(x, y, at_z(s), c),
        ))
    for i, s in enumerate((1, 3)):
        ux_copies.append(remote(
            ux.at[pl.ds(XFIRST[i] + 64 * i, 64)], ux.at[pl.ds(XFIRST[2] + 64 * i, 64)],
            ux_send.at[2 + i], ux_rcv.at[2 + i], dev(at_x(s), y, z, c),
        ))
    for i, s in enumerate((1, -1)):
        uz_copies.append(remote(
            uz.at[pl.ds(ZFIRST[i] + 64 * i, 64)], uz.at[pl.ds(ZFIRST[2 + i], 64)],
            uz_send.at[2 + i], uz_rcv.at[2 + i], dev(x, y, at_z(s), c),
        ))
    for copy in ux_copies[:2] + uz_copies[:2] + [up_own]:
        copy.start()
    for copy in tx_copies[:8] + tz_copies[:8] + core_copies:
        copy.start()
    pl.semaphore_wait(far1, 6)
    for to in (
        dev(x, y, at_z(2), c), dev(x, y, at_z(-2), c), dev(x, at_y(2), z, c), dev(x, at_y(-2), z, c)
    ):
        signal(far2, to)
    for copy in tx_copies[8:] + tz_copies[8:]:
        copy.start()
    uc_copies = [
        remote(
            ux.at[pl.ds(XFIRST[i], TOK)], ux.at[pl.ds(XFIRST[i] + TOK, TOK)],
            uc_send.at[i], uc_rcv.at[i], to_core,
        )
        for i in range(3)
    ] + [
        remote(
            uz.at[pl.ds(ZFIRST[i], ZCOUNT[i])], uz.at[pl.ds(ZFIRST[i] + ZCOUNT[i], ZCOUNT[i])],
            uc_send.at[3 + i], uc_rcv.at[3 + i], to_core,
        )
        for i in range(4)
    ]


    load_wc.wait()
    load_ws.wait()
    for b in range(ROWS // 128):
        rows = slice(b * 128, (b + 1) * 128)
        wbuf[h, rows, :] = (wc[rows, :].astype(F32) * ws_ref[b : b + 1, :]).astype(BF16)

    def part(ylo_of, cc, half):
        return wbuf.at[ylo_of * 2 + cc, pl.ds(half * HALF, HALF)]

    left, right, far = lax.rem(ylo + 3, LO), lax.rem(ylo + 1, LO), lax.rem(ylo + 2, LO)
    w_copies = []

    def send_w(which, half, ssem, rsem, to):
        src = part(which, c, half)
        copy = remote(src, src, ssem, rsem, to)
        copy.start()
        w_copies.append(copy)

    send_w(ylo, 0, wsend.at[0], wrcv.at[0], to_right)
    send_w(ylo, 1, wsend.at[3], wrcv.at[3], to_left)
    send_w(ylo, 1, wsend.at[1], wrcv.at[1], to_right)
    send_w(ylo, 0, wsend.at[2], wrcv.at[2], to_left)
    send_w(ylo, 0, wcsend.at[6], wcrcv.at[6], to_core)
    send_w(ylo, 1, wcsend.at[7], wcrcv.at[7], to_core)
    where = ((left, 0), (left, 1), (right, 0), (right, 1), (far, 0), (far, 1), (ylo, 0), (ylo, 1))

    def arrived(i):
        which, half = where[i]
        ref = part(which, c, half)
        remote(ref, ref, wsend.at[i], wrcv.at[i], to_core).wait_recv()

    def arrived_core(i):
        which, half = where[i]
        ref = part(which, oc, half)
        remote(ref, ref, wcsend.at[i], wcrcv.at[i], to_core).wait_recv()

    def pass_on(i):
        which, half = where[i]
        send_w(which, half, wcsend.at[i], wcrcv.at[i], to_core)

    load_tok.wait()
    vacc[...] = jnp.zeros_like(vacc)

    def multiply(i, cc):
        which, half = where[i]
        slot = which * 2 + cc
        lanes = pl.ds(pl.multiple_of(slot * ROWS + half * HALF, HALF), HALF)
        piece = wbuf[slot, half * HALF : (half + 1) * HALF, :]
        vacc[...] += jnp.dot(tok[:, lanes], piece, preferred_element_type=F32)
        tg_ref[:, lanes] = lax.dot_general(
            ux[0:TOK, :], piece, (((1,), (1,)), ((), ())), preferred_element_type=F32
        ).astype(BF16)

    def product(tokens, upstream, first):
        return lax.dot_general(
            tokens[first : first + 256, :], upstream[first : first + 256, :],
            (((0,), (0,)), ((), ())), preferred_element_type=F32,
        )

    def up_pass_on(copy, i):
        copy.wait_recv()
        uc_copies[i].start()

    for i in (0, 1):
        ux_copies[i].wait_recv()
        ux_copies[2 + i].start()
        uc_copies[i].start()
        uz_copies[i].wait_recv()
        uz_copies[2 + i].start()
        uc_copies[3 + i].start()

    pl.semaphore_wait(far2, 4)
    for s in (4, -4):
        signal(far3, dev(x, y, at_z(s), c))
    arrived(0)
    send_w(left, 0, wsend.at[4], wrcv.at[4], to_right)
    pass_on(0)
    arrived(3)
    send_w(right, 1, wsend.at[5], wrcv.at[5], to_left)
    pass_on(3)
    multiply(6, c)
    multiply(7, c)
    for copy in own_copies:
        copy.wait()
    for copy in core_copies + [up_own]:
        copy.wait_recv()
    term_x[...] = product(tx, ux, 0)
    term_z[...] = product(tz, ux, 0)
    ux_copies[2].wait_recv()
    up_pass_on(ux_copies[3], 2)
    up_pass_on(uz_copies[2], 5)
    up_pass_on(uz_copies[3], 6)
    arrived_core(6)
    multiply(6, oc)
    arrived_core(7)
    multiply(7, oc)
    multiply(0, c)
    multiply(3, c)

    def wait_x(i):
        for copy in tx_copies[4 * i : 4 * i + 4] + [uc_copies[i]]:
            copy.wait_recv()

    def wait_z(i):
        for copy in tz_copies[4 * i : 4 * i + 4] + [uc_copies[3 + i]]:
            copy.wait_recv()

    for i in range(2):
        wait_x(i)
        term_x[...] += product(tx, ux, XFIRST[i])
        wait_z(i)
        term_z[...] += product(tz, uz, ZFIRST[i])

    def of_x(term, xx):
        rows = [term[pl.ds(pl.multiple_of(a * 32 + xx * 8, 8), 8), :] for a in range(8)]
        return jnp.concatenate(rows, axis=0)

    wait_x(2)
    term_x[...] += product(tx, ux, XFIRST[2])
    zout_copies = []
    for i, s in enumerate((2, 1, -1)):
        zout[i] = of_x(term_x, lax.rem(at_z(s), LO)).astype(BF16)
        if s == 2:
            pieces = ((0, 32, 2, 2, 2), (32, 32, -2, 2, 3))
        else:
            pieces = ((0, 64, s, 0 if s == 1 else 1, 0 if s == 1 else 1),)
        for first, count, step, slot, sem in pieces:
            copy = remote(
                zout.at[i, pl.ds(first, count)], zin.at[slot, pl.ds(first, count)],
                z_send.at[sem], z_rcv.at[sem], dev(x, y, at_z(step), c),
            )
            copy.start()
            zout_copies.append(copy)
    wait_z(2)
    wait_z(3)
    term_z[...] += product(tz, uz, ZFIRST[2])
    xout_copies = []
    for i, s in enumerate((2, 1, 3)):
        xout[i] = of_x(term_z, at_x(s)).astype(BF16)
        copy = remote(
            xout.at[i], xin.at[i], x_send.at[i], x_rcv.at[i], dev(at_x(s), y, z, c)
        )
        copy.start()
        xout_copies.append(copy)
    zown[...] = of_x(term_x, klass)
    xown[...] = of_x(term_z, x)

    pl.semaphore_wait(far3, 2)
    for s in range(1, NX):
        signal(far4, dev(at_x(s), y, z, c))
    arrived(1)
    pass_on(1)
    arrived(2)
    pass_on(2)
    multiply(1, c)
    multiply(2, c)
    arrived_core(0)
    multiply(0, oc)
    arrived_core(3)
    multiply(3, oc)

    upper = lax.broadcasted_iota(jnp.int32, (8, KV), 0) < 4

    def regroup(total, first_ylo):
        for j in range(2):
            low, high = [], []
            for k in range(2):
                row = j * 32 + k * 16
                a, b = total[row : row + 8, :], total[row + 8 : row + 16, :]
                low.append(jnp.where(upper, a, pltpu.roll(b, 4, 0)))
                high.append(jnp.where(upper, pltpu.roll(a, 4, 0), b))
            ysend[first_ylo + j] = jnp.concatenate(low, axis=0).astype(BF16)
            ysend[LO + first_ylo + j] = jnp.concatenate(high, axis=0).astype(BF16)

    for copy in zout_copies:
        copy.wait_recv()
    regroup(
        (zown[...] + zin[0].astype(F32)) + (zin[1].astype(F32) + zin[2].astype(F32)), 0
    )
    for copy in xout_copies:
        copy.wait_recv()
    regroup(
        (xown[...] + xin[0].astype(F32)) + (xin[1].astype(F32) + xin[2].astype(F32)), 2
    )
    y_copies = []
    for s in (4, 3, 5, 2, 6, 1, 7):
        copy = remote(
            ysend.at[at_y(s)], yrecv.at[s - 1], y_send.at[s - 1], y_rcv.at[s - 1],
            dev(x, at_y(s), z, c),
        )
        copy.start()
        y_copies.append(copy)

    arrived(4)
    pass_on(4)
    arrived(5)
    pass_on(5)
    multiply(4, c)
    multiply(5, c)
    arrived_core(1)
    multiply(1, oc)
    arrived_core(2)
    multiply(2, oc)

    for copy in y_copies:
        copy.wait_recv()
    total = ysend[y].astype(F32)
    for s in range(NY - 1):
        total += yrecv[s].astype(F32)
    narrow = lax.broadcasted_iota(jnp.int32, (8, 128), 0) < 4
    for b in range(2):
        t = [total[8 * b : 8 * b + 8, 128 * j : 128 * j + 128] for j in range(4)]
        r = [pltpu.roll(a, 4, 0) for a in t]
        low = [jnp.where(narrow, t[j], r[j + 1]) for j in (0, 2)]
        high = [jnp.where(narrow, r[j], t[j + 1]) for j in (0, 2)]
        fsend[2 * b] = jnp.concatenate(low, axis=0).astype(BF16)
        fsend[2 * b + 1] = jnp.concatenate(high, axis=0).astype(BF16)
    pl.semaphore_wait(far4, NX - 1)
    f_copies = []
    for i in range(LO):
        copy = remote(
            fsend.at[i], frecv.at[z // LO], f_send.at[i], f_rcv.at[z // LO], finals[i]
        )
        f_copies.append(copy)

        @pl.when(jnp.logical_not(final_self[i]))
        def _(copy=copy):
            copy.start()

        @pl.when(final_self[i])
        def _(i=i):
            copy = pltpu.make_async_copy(fsend.at[i], frecv.at[z // LO], f_rcv.at[z // LO])
            copy.start()
            copy.wait()

    arrived_core(4)
    multiply(4, oc)
    arrived_core(5)
    multiply(5, oc)
    val_ref[...] = vacc[...].astype(BF16)
    out_copies = [
        pltpu.make_async_copy(tg_ref, tg_hbm, out_sem.at[0]),
        pltpu.make_async_copy(val_ref, val_hbm, out_sem.at[1]),
    ]
    for copy in out_copies:
        copy.start()

    for g in range(4):
        @pl.when(jnp.logical_not(source_self[g]))
        def _(g=g):
            remote(fsend.at[0], frecv.at[g], f_send.at[g], f_rcv.at[g], to_core).wait_recv()

    for copy in (
        core_copies + tx_copies + tz_copies + ux_copies + uz_copies + [up_own] + uc_copies
        + w_copies + zout_copies + xout_copies + y_copies
    ):
        copy.wait_send()
    for i in range(LO):
        @pl.when(jnp.logical_not(final_self[i]))
        def _(i=i):
            f_copies[i].wait_send()
    for copy in out_copies:
        copy.wait()


def writer(val_in, tg_in, last_in, val_out, tg_out, wg_out, val, tg, last, wg, in_sem, out_sem):
    pieces = [(last_in, last, wg_out), (val_in, val, val_out)]
    for i in range(4):
        rows = pl.ds(i * (TOK // 4), TOK // 4)
        pieces.append((tg_in.at[rows], tg.at[rows], tg_out.at[rows]))
    ins = [pltpu.make_async_copy(a, b, in_sem.at[i]) for i, (a, b, _) in enumerate(pieces)]
    outs = [
        pltpu.make_async_copy(wg if i == 0 else b, c, out_sem.at[i])
        for i, (_, b, c) in enumerate(pieces)
    ]
    for copy in ins:
        copy.start()
    ins[0].wait()
    final = (last[0].astype(F32) + last[1].astype(F32)) + (
        last[2].astype(F32) + last[3].astype(F32)
    )
    for j in range(2):
        block = final[8 * j : 8 * j + 8, :]
        wg[:, 256 * j : 256 * j + 128] = block[0:4, :]
        wg[:, 256 * j + 128 : 256 * j + 256] = pltpu.roll(block, 4, 0)[0:4, :]
    outs[0].start()
    for i in range(1, len(ins)):
        ins[i].wait()
        outs[i].start()
    for copy in outs:
        copy.wait()


def write_out(results):
    any_space = pl.BlockSpec(memory_space=pltpu.HBM)
    shapes = (((TOK, KV), BF16), ((TOK, D), BF16), ((4, KV), F32))
    return pl.pallas_call(
        writer,
        out_shape=tuple(jax.ShapeDtypeStruct(*shape) for shape in shapes),
        in_specs=[any_space] * 3,
        out_specs=(any_space,) * 3,
        scratch_shapes=[
            pltpu.VMEM((TOK, KV), BF16),
            pltpu.VMEM((TOK, D), BF16),
            pltpu.VMEM((4, 16, 128), BF16),
            pltpu.VMEM((4, KV), F32),
        ]
        + [pltpu.SemaphoreType.DMA((6,))] * 2,
        compiler_params=pltpu.CompilerParams(vmem_limit_bytes=60 * 1024 * 1024),
    )(*results)


def body(tokens, weight_codes, weight_scales, grad_codes, grad_scales):
    any_space = pl.BlockSpec(memory_space=pltpu.HBM)
    dma = pltpu.SemaphoreType.DMA
    results = pl.pallas_call(
        kernel,
        out_shape=(
            jax.ShapeDtypeStruct((TOK, KV), BF16),
            jax.ShapeDtypeStruct((TOK, D), BF16),
            jax.ShapeDtypeStruct((4, 16, 128), BF16),
        ),
        in_specs=[any_space] * 5,
        out_specs=(any_space, any_space, any_space),
        scratch_shapes=[
            pltpu.VMEM((TOK, KV), BF16),
            pltpu.VMEM((TOK, D), BF16),
            pltpu.VMEM((TOK, D), BF16),
            pltpu.VMEM((ROWS, KV), jnp.int32),
            pltpu.VMEM((TOK, KV), jnp.int32),
            pltpu.VMEM((8, ROWS, KV), BF16),
            pltpu.VMEM((1024, 256), BF16),
            pltpu.VMEM((1024, 256), BF16),
            pltpu.VMEM((1024, KV), BF16),
            pltpu.VMEM((1024, KV), BF16),
            pltpu.VMEM((TOK, KV), F32),
            pltpu.VMEM((256, KV), F32),
            pltpu.VMEM((256, KV), F32),
            pltpu.VMEM((3, 64, KV), BF16),
            pltpu.VMEM((3, 64, KV), BF16),
            pltpu.VMEM((64, KV), F32),
            pltpu.VMEM((3, 64, KV), BF16),
            pltpu.VMEM((3, 64, KV), BF16),
            pltpu.VMEM((64, KV), F32),
            pltpu.VMEM((NY, 16, KV), BF16),
            pltpu.VMEM((NY - 1, 16, KV), BF16),
            pltpu.VMEM((4, 16, 128), BF16),
            pltpu.VMEM((ROWS // 128, KV), F32),
            pltpu.VMEM((HEADS, TOK), F32),
        ]
        + [
            dma((n,))
            for n in (5, 4, 4, 4, 12, 12, 16, 16, 4, 4, 4, 4, 8, 8, 6, 6, 8, 8, 4, 4, 3, 3, 7, 7, 4, 4, 2)
        ]
        + [pltpu.SemaphoreType.REGULAR] * 4,
        compiler_params=pltpu.CompilerParams(
            collective_id=0, has_side_effects=True, vmem_limit_bytes=60 * 1024 * 1024
        ),
    )(tokens, weight_codes, weight_scales, grad_codes, grad_scales.T)
    return write_out(results)


def solution(mesh):
    return jax.shard_map(
        body,
        mesh=mesh,
        in_specs=(
            P(("hst", "outer"), None),
            P("hst", None),
            P("hst", None),
            P(("hst", "outer"), None),
            P(("hst", "outer"), None),
        ),
        out_specs=(P(("hst", "outer"), None), P(("hst", "outer"), None), P(("hst", "outer"), None)),
        check_vma=False,
    )
```

```python
import jax
import jax.numpy as jnp
from jax import lax
from jax.experimental import pallas as pl
from jax.experimental.pallas import tpu as pltpu
from jax.sharding import PartitionSpec as P

F32, BF16 = jnp.float32, jnp.bfloat16
NX, NY, NZ = 4, 8, 16
LO = 4
TOK, D, KV, ROWS, HEADS = 128, 4096, 512, 512, 4
HALF = ROWS // 2
XSTEPS, XFIRST, XCOUNT = (1, 3, 2), (256, 512, 768), (128, 128, 128)
ZSTEPS, ZFIRST, ZCOUNT = (1, -1, 2, -2), (256, 512, 768, 896), (128, 128, 64, 64)


def kernel(
    tok_hbm, wc_hbm, ws_hbm, gc_hbm, gs_hbm,
    val_hbm, tg_hbm, frecv,
    val_ref, tg_ref, tok, tokp, wc, gc, wbuf, tx, tz, ux, uz, vacc, term_x, term_z,
    zout, zin, zown, xout, xin, xown, ysend, yrecv, fsend, ws_ref, gs_ref,
    in_sem, own_sem, core_tsend, core_trcv, tx_send, tx_rcv, tz_send, tz_rcv,
    ux_send, ux_rcv, uz_send, uz_rcv, uc_send, uc_rcv,
    wsend, wrcv, wcsend, wcrcv, z_send, z_rcv, x_send, x_rcv, y_send, y_rcv, f_send, f_rcv, out_sem, far1, far2, far3,
):
    h, o = lax.axis_index("hst"), lax.axis_index("outer")
    c, ylo = lax.rem(h, 2), h // 2
    yhi, x, z = lax.rem(o, 2), lax.rem(o // 2, NX), o // (2 * NX)
    y = yhi * LO + ylo
    oc = 1 - c
    klass = lax.rem(z, LO)

    def dev(x, y, z, c):
        return (lax.rem(y, LO) * 2 + c, (z * NX + x) * 2 + y // LO)

    def at_z(step):
        return lax.rem(z + step + NZ, NZ)

    def at_y(step):
        return lax.rem(y + step + NY, NY)

    def at_x(step):
        return lax.rem(x + step, NX)

    def remote(src, dst, ssem, rsem, to):
        return pltpu.make_async_remote_copy(
            src_ref=src, dst_ref=dst, send_sem=ssem, recv_sem=rsem,
            device_id=to, device_id_type=pl.DeviceIdType.MESH,
        )

    def signal(sem, to):
        pl.semaphore_signal(sem, inc=1, device_id=to, device_id_type=pl.DeviceIdType.MESH)

    finals = [dev(x, y, klass * LO + i, c) for i in range(LO)]
    final_self = [klass * LO + i == z for i in range(LO)]
    source_self = [z // LO + LO * g == z for g in range(4)]
    to_left, to_right = dev(x, at_y(-1), z, c), dev(x, at_y(1), z, c)

    barrier = pltpu.get_barrier_semaphore()
    partners = [dev(at_x(s), y, z, cc) for s in (1, 3) for cc in (c, oc)]
    partners += [dev(x, y, at_z(s), cc) for s in (1, -1) for cc in (c, oc)]
    partners += [dev(x, at_y(1), z, c), dev(x, at_y(-1), z, c), dev(x, y, z, oc)]
    for p in partners:
        signal(barrier, p)

    load_tok = pltpu.make_async_copy(tok_hbm, tok, in_sem.at[0])
    load_wc = pltpu.make_async_copy(wc_hbm, wc, in_sem.at[1])
    load_gc = pltpu.make_async_copy(gc_hbm, gc, in_sem.at[2])
    load_gs = pltpu.make_async_copy(gs_hbm, gs_ref, in_sem.at[3])
    load_ws = pltpu.make_async_copy(ws_hbm, ws_ref, in_sem.at[4])
    for copy in (load_gc, load_gs, load_wc, load_ws, load_tok):
        copy.start()

    def columns(ylo_of, cc, q):
        return pl.ds(pl.multiple_of(((ylo_of * 2 + cc) * 4 + q) * 128, 128), 128)

    own_copies = []
    for j in range(2):
        lanes = pl.ds(j * 128, 128)
        own_copies.append(pltpu.make_async_copy(
            tok_hbm.at[:, columns(2 + j, c, klass)], tz.at[pl.ds(0, TOK), lanes], own_sem.at[2 + j]
        ))
    for copy in own_copies:
        copy.start()

    load_gc.wait()
    load_gs.wait()
    scales = gs_ref[...].T
    for k in range(HEADS):
        lanes = slice(k * 128, (k + 1) * 128)
        ux[0:TOK, lanes] = (gc[:, lanes].astype(F32) * scales[:, k : k + 1]).astype(BF16)
    load_tok.wait()
    new = lax.broadcasted_iota(jnp.int32, (ROWS, ROWS), 1)
    old = lax.broadcasted_iota(jnp.int32, (ROWS, ROWS), 0)
    source = ((new & 127) >> 3) * 32 + (new >> 7) * 8 + (new & 7)
    permute = jnp.where(old == source, 1.0, 0.0).astype(BF16)
    for j in range(2):
        for k in range(2):
            first = (2 * j + k) * ROWS
            mixed = jnp.dot(
                tok[:, first : first + ROWS], permute, preferred_element_type=F32
            ).astype(BF16)
            for xx in range(NX):
                tokp[k, :, xx * 256 + j * 128 : xx * 256 + (j + 1) * 128] = mixed[
                    :, xx * 128 : (xx + 1) * 128
                ]
    pl.semaphore_wait(barrier, len(partners))
    for to in (
        dev(x, y, at_z(1), c), dev(x, y, at_z(-1), c), dev(at_x(1), y, z, c), dev(at_x(3), y, z, c),
        to_left, to_right,
    ):
        signal(far1, to)

    def of_owner(xx):
        return pl.ds(pl.multiple_of(xx * 256, 256), 256)

    core_copies, tx_copies, tz_copies = [], [], []
    for j in range(2):
        lanes = pl.ds(j * 128, 128)
        core_copies.append(remote(
            tok_hbm.at[:, columns(2 + j, oc, klass)], tz.at[pl.ds(TOK, TOK), lanes],
            core_tsend.at[2 + j], core_trcv.at[2 + j], dev(x, y, z, oc),
        ))
    for i, s in enumerate(XSTEPS):
        for k, cc in enumerate((c, oc)):
            tx_copies.append(remote(
                tokp.at[cc, :, of_owner(at_x(s))],
                tx.at[pl.ds(XFIRST[i] + k * XCOUNT[i], XCOUNT[i])],
                tx_send.at[2 * i + k], tx_rcv.at[2 * i + k], dev(at_x(s), y, z, cc),
            ))
    own_x = pltpu.make_async_copy(
        tokp.at[c, :, of_owner(x)], tx.at[pl.ds(0, TOK)], own_sem.at[0]
    )
    core_x = remote(
        tokp.at[oc, :, of_owner(x)], tx.at[pl.ds(TOK, TOK)],
        core_tsend.at[0], core_trcv.at[0], dev(x, y, z, oc),
    )
    for i, s in enumerate(ZSTEPS):
        first = 64 if s == -2 else 0
        for k, cc in enumerate((c, oc)):
            for j in range(2):
                tz_copies.append(remote(
                    tok_hbm.at[pl.ds(first, ZCOUNT[i]), columns(2 + j, cc, lax.rem(at_z(s), LO))],
                    tz.at[pl.ds(ZFIRST[i] + k * ZCOUNT[i], ZCOUNT[i]), pl.ds(j * 128, 128)],
                    tz_send.at[4 * i + 2 * k + j], tz_rcv.at[4 * i + 2 * k + j],
                    dev(x, y, at_z(s), cc),
                ))

    to_core = dev(x, y, z, oc)
    up_own = remote(
        ux.at[pl.ds(0, TOK)], ux.at[pl.ds(TOK, TOK)], uc_send.at[7], uc_rcv.at[7], to_core
    )
    ux_copies, uz_copies = [], []
    for i, s in enumerate((1, 3)):
        ux_copies.append(remote(
            ux.at[pl.ds(0, TOK)], ux.at[pl.ds(XFIRST[i], TOK)],
            ux_send.at[i], ux_rcv.at[i], dev(at_x(s), y, z, c),
        ))
    for i, s in enumerate((1, -1)):
        uz_copies.append(remote(
            ux.at[pl.ds(0, TOK)], uz.at[pl.ds(ZFIRST[i], TOK)],
            uz_send.at[i], uz_rcv.at[i], dev(x, y, at_z(s), c),
        ))
    for i, s in enumerate((1, 3)):
        ux_copies.append(remote(
            ux.at[pl.ds(XFIRST[i] + 64 * i, 64)], ux.at[pl.ds(XFIRST[2] + 64 * i, 64)],
            ux_send.at[2 + i], ux_rcv.at[2 + i], dev(at_x(s), y, z, c),
        ))
    for i, s in enumerate((1, -1)):
        uz_copies.append(remote(
            uz.at[pl.ds(ZFIRST[i] + 64 * i, 64)], uz.at[pl.ds(ZFIRST[2 + i], 64)],
            uz_send.at[2 + i], uz_rcv.at[2 + i], dev(x, y, at_z(s), c),
        ))
    for copy in ux_copies[:2] + uz_copies[:2] + [up_own]:
        copy.start()
    for copy in tz_copies[:8] + core_copies:
        copy.start()
    for copy in tx_copies[:4] + [own_x, core_x]:
        copy.start()
    own_copies.append(own_x)
    core_copies.append(core_x)
    pl.semaphore_wait(far1, 6)
    for to in (
        dev(x, y, at_z(2), c), dev(x, y, at_z(-2), c), dev(x, at_y(2), z, c), dev(x, at_y(-2), z, c)
    ):
        signal(far2, to)
    for copy in tx_copies[4:] + tz_copies[8:]:
        copy.start()
    uc_copies = [
        remote(
            ux.at[pl.ds(XFIRST[i], TOK)], ux.at[pl.ds(XFIRST[i] + TOK, TOK)],
            uc_send.at[i], uc_rcv.at[i], to_core,
        )
        for i in range(3)
    ] + [
        remote(
            uz.at[pl.ds(ZFIRST[i], ZCOUNT[i])], uz.at[pl.ds(ZFIRST[i] + ZCOUNT[i], ZCOUNT[i])],
            uc_send.at[3 + i], uc_rcv.at[3 + i], to_core,
        )
        for i in range(4)
    ]


    load_wc.wait()
    load_ws.wait()
    for b in range(ROWS // 128):
        rows = slice(b * 128, (b + 1) * 128)
        wbuf[h, rows, :] = (wc[rows, :].astype(F32) * ws_ref[b : b + 1, :]).astype(BF16)

    def part(ylo_of, cc, half):
        return wbuf.at[ylo_of * 2 + cc, pl.ds(half * HALF, HALF)]

    left, right, far = lax.rem(ylo + 3, LO), lax.rem(ylo + 1, LO), lax.rem(ylo + 2, LO)
    w_copies = []

    def send_w(which, half, ssem, rsem, to):
        src = part(which, c, half)
        copy = remote(src, src, ssem, rsem, to)
        copy.start()
        w_copies.append(copy)

    send_w(ylo, 0, wsend.at[0], wrcv.at[0], to_right)
    send_w(ylo, 1, wsend.at[3], wrcv.at[3], to_left)
    send_w(ylo, 1, wsend.at[1], wrcv.at[1], to_right)
    send_w(ylo, 0, wsend.at[2], wrcv.at[2], to_left)
    send_w(ylo, 0, wcsend.at[6], wcrcv.at[6], to_core)
    send_w(ylo, 1, wcsend.at[7], wcrcv.at[7], to_core)
    where = ((left, 0), (left, 1), (right, 0), (right, 1), (far, 0), (far, 1), (ylo, 0), (ylo, 1))

    def arrived(i):
        which, half = where[i]
        ref = part(which, c, half)
        remote(ref, ref, wsend.at[i], wrcv.at[i], to_core).wait_recv()

    def arrived_core(i):
        which, half = where[i]
        ref = part(which, oc, half)
        remote(ref, ref, wcsend.at[i], wcrcv.at[i], to_core).wait_recv()

    def pass_on(i):
        which, half = where[i]
        send_w(which, half, wcsend.at[i], wcrcv.at[i], to_core)

    vacc[...] = jnp.zeros_like(vacc)

    def multiply(i, cc):
        which, half = where[i]
        slot = which * 2 + cc
        lanes = pl.ds(pl.multiple_of(slot * ROWS + half * HALF, HALF), HALF)
        piece = wbuf[slot, half * HALF : (half + 1) * HALF, :]
        vacc[...] += jnp.dot(tok[:, lanes], piece, preferred_element_type=F32)
        tg_ref[:, lanes] = lax.dot_general(
            ux[0:TOK, :], piece, (((1,), (1,)), ((), ())), preferred_element_type=F32
        ).astype(BF16)

    def product(tokens, upstream, first):
        return lax.dot_general(
            tokens[first : first + 256, :], upstream[first : first + 256, :],
            (((0,), (0,)), ((), ())), preferred_element_type=F32,
        )

    def up_pass_on(copy, i):
        copy.wait_recv()
        uc_copies[i].start()

    for i in (0, 1):
        ux_copies[i].wait_recv()
        ux_copies[2 + i].start()
        uc_copies[i].start()
        uz_copies[i].wait_recv()
        uz_copies[2 + i].start()
        uc_copies[3 + i].start()

    pl.semaphore_wait(far2, 4)
    for s in (4, -4):
        signal(far3, dev(x, y, at_z(s), c))
    arrived(0)
    send_w(left, 0, wsend.at[4], wrcv.at[4], to_right)
    pass_on(0)
    arrived(3)
    send_w(right, 1, wsend.at[5], wrcv.at[5], to_left)
    pass_on(3)
    multiply(6, c)
    multiply(7, c)
    for copy in own_copies:
        copy.wait()
    for copy in core_copies + [up_own]:
        copy.wait_recv()
    term_x[...] = product(tx, ux, 0)
    term_z[...] = product(tz, ux, 0)
    ux_copies[2].wait_recv()
    up_pass_on(ux_copies[3], 2)
    up_pass_on(uz_copies[2], 5)
    up_pass_on(uz_copies[3], 6)
    arrived_core(6)
    multiply(6, oc)
    arrived_core(7)
    multiply(7, oc)
    multiply(0, c)
    multiply(3, c)

    def wait_x(i):
        for copy in tx_copies[2 * i : 2 * i + 2] + [uc_copies[i]]:
            copy.wait_recv()

    def wait_z(i):
        for copy in tz_copies[4 * i : 4 * i + 4] + [uc_copies[3 + i]]:
            copy.wait_recv()

    for i in range(2):
        wait_x(i)
        term_x[...] += product(tx, ux, XFIRST[i])
        wait_z(i)
        term_z[...] += product(tz, uz, ZFIRST[i])

    def of_x(term, xx):
        rows = [term[pl.ds(pl.multiple_of(a * 32 + xx * 8, 8), 8), :] for a in range(8)]
        return jnp.concatenate(rows, axis=0)

    def of_q(q):
        rows = [term_x[pl.ds(pl.multiple_of(a * 128 + q * 32, 32), 32), :] for a in range(2)]
        return jnp.concatenate(rows, axis=0)

    wait_x(2)
    term_x[...] += product(tx, ux, XFIRST[2])
    zout_copies = []
    for i, s in enumerate((2, 1, -1)):
        zout[i] = of_q(lax.rem(at_z(s), LO)).astype(BF16)
        if s == 2:
            pieces = ((0, 32, 2, 2, 2), (32, 32, -2, 2, 3))
        else:
            pieces = ((0, 64, s, 0 if s == 1 else 1, 0 if s == 1 else 1),)
        for first, count, step, slot, sem in pieces:
            copy = remote(
                zout.at[i, pl.ds(first, count)], zin.at[slot, pl.ds(first, count)],
                z_send.at[sem], z_rcv.at[sem], dev(x, y, at_z(step), c),
            )
            copy.start()
            zout_copies.append(copy)
    wait_z(2)
    wait_z(3)
    term_z[...] += product(tz, uz, ZFIRST[2])
    xout_copies = []
    for i, s in enumerate((2, 1, 3)):
        xout[i] = of_x(term_z, at_x(s)).astype(BF16)
        copy = remote(
            xout.at[i], xin.at[i], x_send.at[i], x_rcv.at[i], dev(at_x(s), y, z, c)
        )
        copy.start()
        xout_copies.append(copy)
    zown[...] = of_q(klass)
    xown[...] = of_x(term_z, x)

    pl.semaphore_wait(far3, 2)
    arrived(1)
    pass_on(1)
    arrived(2)
    pass_on(2)
    multiply(1, c)
    multiply(2, c)
    arrived_core(0)
    multiply(0, oc)
    arrived_core(3)
    multiply(3, oc)

    upper = lax.broadcasted_iota(jnp.int32, (8, KV), 0) < 4

    def regroup(total, first_ylo):
        for j in range(2):
            low, high = [], []
            for k in range(2):
                row = j * 32 + k * 16
                a, b = total[row : row + 8, :], total[row + 8 : row + 16, :]
                low.append(jnp.where(upper, a, pltpu.roll(b, 4, 0)))
                high.append(jnp.where(upper, pltpu.roll(a, 4, 0), b))
            ysend[first_ylo + j] = jnp.concatenate(low, axis=0).astype(BF16)
            ysend[LO + first_ylo + j] = jnp.concatenate(high, axis=0).astype(BF16)

    for copy in zout_copies:
        copy.wait_recv()
    regroup(
        (zown[...] + zin[0].astype(F32)) + (zin[1].astype(F32) + zin[2].astype(F32)), 0
    )
    for copy in xout_copies:
        copy.wait_recv()
    regroup(
        (xown[...] + xin[0].astype(F32)) + (xin[1].astype(F32) + xin[2].astype(F32)), 2
    )
    y_copies = []
    for s in (4, 3, 5, 2, 6, 1, 7):
        copy = remote(
            ysend.at[at_y(s)], yrecv.at[s - 1], y_send.at[s - 1], y_rcv.at[s - 1],
            dev(x, at_y(s), z, c),
        )
        copy.start()
        y_copies.append(copy)

    arrived(4)
    pass_on(4)
    arrived(5)
    pass_on(5)
    multiply(4, c)
    multiply(5, c)
    arrived_core(1)
    multiply(1, oc)
    arrived_core(2)
    multiply(2, oc)

    for copy in y_copies:
        copy.wait_recv()
    total = ysend[y].astype(F32)
    for s in range(NY - 1):
        total += yrecv[s].astype(F32)
    narrow = lax.broadcasted_iota(jnp.int32, (8, 128), 0) < 4
    for b in range(2):
        t = [total[8 * b : 8 * b + 8, 128 * j : 128 * j + 128] for j in range(4)]
        r = [pltpu.roll(a, 4, 0) for a in t]
        low = [jnp.where(narrow, t[j], r[j + 1]) for j in (0, 2)]
        high = [jnp.where(narrow, r[j], t[j + 1]) for j in (0, 2)]
        fsend[2 * b] = jnp.concatenate(low, axis=0).astype(BF16)
        fsend[2 * b + 1] = jnp.concatenate(high, axis=0).astype(BF16)
    f_copies = []
    for i in range(LO):
        copy = remote(
            fsend.at[i], frecv.at[z // LO], f_send.at[i], f_rcv.at[z // LO], finals[i]
        )
        f_copies.append(copy)

        @pl.when(jnp.logical_not(final_self[i]))
        def _(copy=copy):
            copy.start()

        @pl.when(final_self[i])
        def _(i=i):
            copy = pltpu.make_async_copy(fsend.at[i], frecv.at[z // LO], f_rcv.at[z // LO])
            copy.start()
            copy.wait()

    arrived_core(4)
    multiply(4, oc)
    arrived_core(5)
    multiply(5, oc)
    val_ref[...] = vacc[...].astype(BF16)
    out_copies = [
        pltpu.make_async_copy(tg_ref, tg_hbm, out_sem.at[0]),
        pltpu.make_async_copy(val_ref, val_hbm, out_sem.at[1]),
    ]
    for copy in out_copies:
        copy.start()

    for g in range(4):
        @pl.when(jnp.logical_not(source_self[g]))
        def _(g=g):
            remote(fsend.at[0], frecv.at[g], f_send.at[g], f_rcv.at[g], to_core).wait_recv()

    for copy in (
        core_copies + tx_copies + tz_copies + ux_copies + uz_copies + [up_own] + uc_copies
        + w_copies + zout_copies + xout_copies + y_copies
    ):
        copy.wait_send()
    for i in range(LO):
        @pl.when(jnp.logical_not(final_self[i]))
        def _(i=i):
            f_copies[i].wait_send()
    for copy in out_copies:
        copy.wait()


def writer(val_in, tg_in, last_in, val_out, tg_out, wg_out, val, tg, last, wg, in_sem, out_sem):
    pieces = [(last_in, last, wg_out), (val_in, val, val_out)]
    for i in range(4):
        rows = pl.ds(i * (TOK // 4), TOK // 4)
        pieces.append((tg_in.at[rows], tg.at[rows], tg_out.at[rows]))
    ins = [pltpu.make_async_copy(a, b, in_sem.at[i]) for i, (a, b, _) in enumerate(pieces)]
    outs = [
        pltpu.make_async_copy(wg if i == 0 else b, c, out_sem.at[i])
        for i, (_, b, c) in enumerate(pieces)
    ]
    for copy in ins:
        copy.start()
    ins[0].wait()
    final = (last[0].astype(F32) + last[1].astype(F32)) + (
        last[2].astype(F32) + last[3].astype(F32)
    )
    for j in range(2):
        block = final[8 * j : 8 * j + 8, :]
        wg[:, 256 * j : 256 * j + 128] = block[0:4, :]
        wg[:, 256 * j + 128 : 256 * j + 256] = pltpu.roll(block, 4, 0)[0:4, :]
    outs[0].start()
    for i in range(1, len(ins)):
        ins[i].wait()
        outs[i].start()
    for copy in outs:
        copy.wait()


def write_out(results):
    any_space = pl.BlockSpec(memory_space=pltpu.HBM)
    shapes = (((TOK, KV), BF16), ((TOK, D), BF16), ((4, KV), F32))
    return pl.pallas_call(
        writer,
        out_shape=tuple(jax.ShapeDtypeStruct(*shape) for shape in shapes),
        in_specs=[any_space] * 3,
        out_specs=(any_space,) * 3,
        scratch_shapes=[
            pltpu.VMEM((TOK, KV), BF16),
            pltpu.VMEM((TOK, D), BF16),
            pltpu.VMEM((4, 16, 128), BF16),
            pltpu.VMEM((4, KV), F32),
        ]
        + [pltpu.SemaphoreType.DMA((6,))] * 2,
        compiler_params=pltpu.CompilerParams(vmem_limit_bytes=60 * 1024 * 1024),
    )(*results)


def body(tokens, weight_codes, weight_scales, grad_codes, grad_scales):
    any_space = pl.BlockSpec(memory_space=pltpu.HBM)
    dma = pltpu.SemaphoreType.DMA
    results = pl.pallas_call(
        kernel,
        out_shape=(
            jax.ShapeDtypeStruct((TOK, KV), BF16),
            jax.ShapeDtypeStruct((TOK, D), BF16),
            jax.ShapeDtypeStruct((4, 16, 128), BF16),
        ),
        in_specs=[any_space] * 5,
        out_specs=(any_space, any_space, any_space),
        scratch_shapes=[
            pltpu.VMEM((TOK, KV), BF16),
            pltpu.VMEM((TOK, D), BF16),
            pltpu.VMEM((TOK, D), BF16),
            pltpu.VMEM((2, TOK, 1024), BF16),
            pltpu.VMEM((ROWS, KV), jnp.int32),
            pltpu.VMEM((TOK, KV), jnp.int32),
            pltpu.VMEM((8, ROWS, KV), BF16),
            pltpu.VMEM((1024, 256), BF16),
            pltpu.VMEM((1024, 256), BF16),
            pltpu.VMEM((1024, KV), BF16),
            pltpu.VMEM((1024, KV), BF16),
            pltpu.VMEM((TOK, KV), F32),
            pltpu.VMEM((256, KV), F32),
            pltpu.VMEM((256, KV), F32),
            pltpu.VMEM((3, 64, KV), BF16),
            pltpu.VMEM((3, 64, KV), BF16),
            pltpu.VMEM((64, KV), F32),
            pltpu.VMEM((3, 64, KV), BF16),
            pltpu.VMEM((3, 64, KV), BF16),
            pltpu.VMEM((64, KV), F32),
            pltpu.VMEM((NY, 16, KV), BF16),
            pltpu.VMEM((NY - 1, 16, KV), BF16),
            pltpu.VMEM((4, 16, 128), BF16),
            pltpu.VMEM((ROWS // 128, KV), F32),
            pltpu.VMEM((HEADS, TOK), F32),
        ]
        + [
            dma((n,))
            for n in (5, 4, 4, 4, 12, 12, 16, 16, 4, 4, 4, 4, 8, 8, 6, 6, 8, 8, 4, 4, 3, 3, 7, 7, 4, 4, 2)
        ]
        + [pltpu.SemaphoreType.REGULAR] * 3,
        compiler_params=pltpu.CompilerParams(
            collective_id=0, has_side_effects=True, vmem_limit_bytes=60 * 1024 * 1024
        ),
    )(tokens, weight_codes, weight_scales, grad_codes, grad_scales.T)
    return write_out(results)


def solution(mesh):
    return jax.shard_map(
        body,
        mesh=mesh,
        in_specs=(
            P(("hst", "outer"), None),
            P("hst", None),
            P("hst", None),
            P(("hst", "outer"), None),
            P(("hst", "outer"), None),
        ),
        out_specs=(P(("hst", "outer"), None), P(("hst", "outer"), None), P(("hst", "outer"), None)),
        check_vma=False,
    )
```
